256 devices in a mesh: leaf: 64 (over x_lo, z, y), rhs: 4 (over x_hi, core).
Axes of the slice: x: 4 (x_hi: 2, x_lo: 2; x = x_hi * 2 + x_lo), y: 4, z: 8, core: 2. Of those that a mesh axis runs over, the one named last changes fastest.
Arguments:
- rhs_block: bfloat16 [128, 262144], P('rhs', 'leaf'), may hold values from -6 to 6
- col_basis: bfloat16 [64, 262144], P(None, 'leaf'), may hold values from -0.25 to 0.25
- row_basis: bfloat16 [64, 262144], P(None, 'leaf'), may hold values from -0.75 to 0.75
- leaf_transfer: float32 [512, 64, 64], P('leaf'), may hold values from -0.5 to 0.5
- leaf_coupling: float32 [512, 64, 64], P('leaf'), may hold values from -0.75 to 0.75
- inner_transfer: float32 [64, 6, 64, 64], P('leaf'), may hold values from -0.5 to 0.5
- inner_coupling: float32 [64, 6, 64, 64], P('leaf'), may hold values from -0.75 to 0.75
- tree_transfer: float32 [126, 64, 64], replicated, may hold values from -0.5 to 0.5
- tree_coupling: float32 [126, 64, 64], replicated, may hold values from -0.75 to 0.75
- diag_blocks: bfloat16 [512, 512, 512], P('leaf', 'rhs'), may hold values from -0.25 to 0.25
- near_blocks: bfloat16 [512, 2, 512, 512], P('leaf', None, 'rhs'), may hold values from -0.25 to 0.25
- near_leaves: int32 [512, 2], P('leaf'), may hold values from 0 to 511, as said below
Outputs:
- product: float32 [128, 262144], P('rhs', 'leaf')
The draws below stay inside these ranges and needn't reach their ends.
Inputs may be any that keep to these rules, and one draw needn't show every extreme that they name: `near_leaves`: each entry names another leaf that lies at most 2 leaves from its own leaf; the 2 entries of a leaf differ unless the grid's end folds them together.
All inputs are finite; a program needn't handle non-finite values.
Results may differ from the reference program's by a relative error of at most 0.0021.
Values may be sent and summed in bfloat16 or wider, within the bound.
No kernel may reach another device: no remote copies, remote signals or barrier semaphores. Data moves between devices by JAX's collectives and lax.ppermute only.
A program may use at most 128 MiB of HBM per device.

```python
import jax
import jax.numpy as jnp
from jax import lax

M = 512
K = 64
RHS = 128
LEAF_DEV = 8
NEAR = 2
LEAVES = 512
POINTS = 262144
NODES = 126
N_LEAF = 64


def draw_near_leaves(key, part):
    key = jax.random.fold_in(key, 5)
    scores = jax.random.randint(key, (LEAVES, 4), 0, 1 << 20) * 4 + jnp.arange(4, dtype=jnp.int32)
    order = jnp.argsort(scores, axis=1)[:, :NEAR]
    offsets = jnp.array([-2, -1, 1, 2], jnp.int32)[order]
    base = jnp.arange(LEAVES, dtype=jnp.int32)[:, None]
    ahead = base + offsets
    inside = (ahead >= 0) & (ahead < LEAVES)
    return jnp.where(inside, ahead, base - offsets).astype(jnp.int32)


def levels(own_key, shape, split, low, top_value):
    def one(position, shards_of):
        draws = jax.random.uniform(jax.random.fold_in(jax.random.fold_in(own_key, 6), position), (shards_of,), jnp.float32, low / len(split), top_value / len(split))
        return jnp.repeat(jnp.exp(draws), shape[position] // shards_of).reshape((-1,) + (1,) * (len(shape) - position - 1))

    loudness = one(*split[0])
    for cut in split[1:]:
        loudness = loudness * one(*cut)
    return loudness


def normal_values(key, extent, width, most, pieces=(), kind=jnp.bfloat16):
    factor_of = levels(key, extent, pieces, -0.22, 0.18) if pieces else 1.0
    values = jax.random.normal(key, extent, jnp.float32) * width * factor_of
    return jnp.minimum(jnp.maximum(values, -most), most).astype(kind)


def setup_inputs(seed: int = 0) -> dict:
    streams_of = jax.random.split(jax.random.key(seed), 13)
    rhs_block = normal_values(streams_of[0], (RHS, POINTS), 1.0, 6.0, ((0, 4), (1, 64)))
    col_basis = normal_values(streams_of[1], (K, POINTS), M ** -0.5, 0.25, ((1, 64),))
    row_basis = normal_values(streams_of[2], (K, POINTS), K ** -0.5, 0.75, ((1, 64),))
    leaf_transfer = normal_values(streams_of[3], (LEAVES, K, K), (2 * K) ** -0.5, 0.5, ((0, 64),), jnp.float32)
    leaf_coupling = normal_values(streams_of[4], (LEAVES, K, K), K ** -0.5, 0.75, ((0, 64),), jnp.float32)
    inner_transfer = normal_values(streams_of[5], (N_LEAF, LEAF_DEV - 2, K, K), (2 * K) ** -0.5, 0.5, ((0, 64),), jnp.float32)
    inner_coupling = normal_values(streams_of[6], (N_LEAF, LEAF_DEV - 2, K, K), K ** -0.5, 0.75, ((0, 64),), jnp.float32)
    tree_transfer = normal_values(streams_of[7], (NODES, K, K), (2 * K) ** -0.5, 0.5, (), jnp.float32)
    tree_coupling = normal_values(streams_of[8], (NODES, K, K), K ** -0.5, 0.75, (), jnp.float32)
    diag_blocks = normal_values(streams_of[9], (LEAVES, M, M), M ** -0.5, 0.25, ((0, 64), (1, 4)))
    near_blocks = normal_values(streams_of[10], (LEAVES, NEAR, M, M), M ** -0.5, 0.25, ((0, 64), (2, 4)))
    near_leaves = draw_near_leaves(jax.random.fold_in(streams_of[12], 71), 0)
    return dict(rhs_block=rhs_block, col_basis=col_basis, row_basis=row_basis, leaf_transfer=leaf_transfer, leaf_coupling=leaf_coupling, inner_transfer=inner_transfer, inner_coupling=inner_coupling, tree_transfer=tree_transfer, tree_coupling=tree_coupling, diag_blocks=diag_blocks, near_blocks=near_blocks, near_leaves=near_leaves)


HIGH = lax.Precision.HIGHEST


def flip_pairs(values):
    count = values.shape[0]
    return values.reshape((count // 2, 2) + values.shape[1:])[:, ::-1].reshape(values.shape)


def level_mats(inner, tree, count):
    if count > N_LEAF:
        depth = (count // N_LEAF).bit_length() - 1
        low = 2 ** depth - 2
        return inner[:, low:low + 2 ** depth].reshape(count, K, K)
    return tree[count - 2:2 * count - 2]


def reference(rhs_block, col_basis, row_basis, leaf_transfer, leaf_coupling, inner_transfer, inner_coupling, tree_transfer, tree_coupling, diag_blocks, near_blocks, near_leaves):
    leaves = LEAVES
    inputs = rhs_block.reshape(RHS, leaves, M).astype(jnp.float32)
    columns = col_basis.reshape(K, leaves, M).astype(jnp.float32)
    coeffs = jnp.einsum("rlm,klm->lrk", inputs, columns, precision=HIGH)
    leaf_terms = jnp.einsum("lrj,lkj->lrk", flip_pairs(coeffs), leaf_coupling, precision=HIGH)
    lifted = jnp.einsum("lrk,lkj->lrj", coeffs, leaf_transfer, precision=HIGH)
    current = lifted.reshape(leaves // 2, 2, RHS, K).sum(1)
    count = leaves // 2
    couplings = []
    while count >= 2:
        matrices = level_mats(inner_coupling, tree_coupling, count)
        couplings.append(jnp.einsum("nrj,nkj->nrk", flip_pairs(current), matrices, precision=HIGH))
        if count > 2:
            transfers = level_mats(inner_transfer, tree_transfer, count)
            lifted = jnp.einsum("nrk,nkj->nrj", current, transfers, precision=HIGH)
            current = lifted.reshape(count // 2, 2, RHS, K).sum(1)
        count = count // 2
    down = couplings[-1]
    count = 4
    for level in range(len(couplings) - 2, -1, -1):
        transfers = level_mats(inner_transfer, tree_transfer, count)
        down = couplings[level] + jnp.einsum("nrj,nkj->nrk", jnp.repeat(down, 2, axis=0), transfers, precision=HIGH)
        count = count * 2
    leaf_down = leaf_terms + jnp.einsum("lrj,lkj->lrk", jnp.repeat(down, 2, axis=0), leaf_transfer, precision=HIGH)
    rounded = leaf_down.astype(jnp.bfloat16).astype(jnp.float32)
    rows = row_basis.reshape(K, leaves, M).astype(jnp.float32)
    far = jnp.einsum("lrk,klm->rlm", rounded, rows, precision=HIGH)
    near = jnp.einsum("lmn,rln->rlm", diag_blocks.astype(jnp.float32), inputs, precision=HIGH)
    picked = inputs[:, near_leaves]
    near = near + jnp.einsum("ljmn,rljn->rlm", near_blocks.astype(jnp.float32), picked, precision=HIGH)
    return (far + near).reshape(RHS, POINTS)
```

```python
import functools

import jax
import jax.numpy as jnp
from jax import lax
from jax.experimental import pallas as pl
from jax.experimental.pallas import tpu as pltpu
from jax.sharding import PartitionSpec as P

HIGH = lax.Precision.HIGHEST
F32 = jnp.float32
BF16 = jnp.bfloat16
VMEM = pl.BlockSpec(memory_space=pltpu.VMEM)
ANY = pl.BlockSpec(memory_space=pl.ANY)
PLAIN = (((1,), (0,)), ((), ()))
TURNED = (((1,), (1,)), ((), ()))


def halves(x):
    top = x.astype(BF16)
    return top, (x - top.astype(F32)).astype(BF16)


def dot3(a, b, dims=PLAIN):
    ah, al = halves(a)
    bh, bl = halves(b)
    dot = functools.partial(lax.dot_general, dimension_numbers=dims, preferred_element_type=F32)
    return dot(ah, bh) + (dot(ah, bl) + dot(al, bh))


def swapped(x, axis, bit):
    count = lax.axis_size(axis)
    return lax.ppermute(x, axis, [(i, i ^ bit) for i in range(count)])


def limit(mib):
    return pltpu.CompilerParams(vmem_limit_bytes=mib << 20)


def in_hbm(x):
    return pltpu.with_memory_space_constraint(x, pltpu.HBM)


def fetched(pairs, sems):
    copies = []
    for at, (source, target) in enumerate(pairs):
        copy = pltpu.make_async_copy(source, target, sems.at[at])
        copy.start()
        copies.append(copy)
    return copies


def up_kernel(
    rhs_hbm, cols_hbm, leaf_hbm, inner_hbm, coeffs, second, first, block, rhs, cols, leaf_tr, inner_tr, sems
):
    half = rhs.shape[1] // 2
    size = rhs.shape[1] // 8
    pairs = []
    for side in range(2):
        span = pl.ds(side * half, half)
        pairs += [(rhs_hbm.at[:, span], rhs.at[:, span]), (cols_hbm.at[:, span], cols.at[:, span])]
    pairs += [(leaf_hbm, leaf_tr), (inner_hbm, inner_tr)]
    copies = fetched(pairs, sems)
    parts = []
    for leaf in range(8):
        if leaf % 4 == 0:
            copies[leaf // 2].wait()
            copies[leaf // 2 + 1].wait()
        span = slice(leaf * size, (leaf + 1) * size)
        parts.append(
            lax.dot_general(rhs[:, span], cols[:, span], TURNED, preferred_element_type=F32)
        )
    copies[4].wait()
    copies[5].wait()
    ups = []
    for pair in range(4):
        both = jnp.concatenate(parts[2 * pair : 2 * pair + 2], axis=1)
        coeffs[:, pair * 128 : (pair + 1) * 128] = both
        ups.append(dot3(both, leaf_tr[pair]))
    left = jnp.concatenate(ups[:2], axis=1)
    right = jnp.concatenate(ups[2:], axis=1)
    second[:, :128] = left
    second[:, 128:] = right
    both = jnp.concatenate([dot3(left, inner_tr[1]), dot3(right, inner_tr[2])], axis=1)
    first[...] = both
    block[...] = dot3(both, inner_tr[0])


def run_up(rhs, cols, leaf_tr, inner_tr):
    rows = rhs.shape[0]
    skel = cols.shape[0]
    return pl.pallas_call(
        up_kernel,
        in_specs=[ANY] * 4,
        out_specs=[VMEM] * 4,
        out_shape=[
            pltpu.VMEM((rows, 8 * skel), F32),
            pltpu.VMEM((rows, 4 * skel), F32),
            pltpu.VMEM((rows, 2 * skel), F32),
            pltpu.VMEM((rows, skel), F32),
        ],
        scratch_shapes=[pltpu.VMEM(x.shape, x.dtype) for x in (rhs, cols, leaf_tr, inner_tr)]
        + [pltpu.SemaphoreType.DMA((6,))],
        compiler_params=limit(4),
        cost_estimate=pl.CostEstimate(flops=200_000_000, bytes_accessed=2_000_000, transcendentals=0),
        name="up",
    )(*map(in_hbm, (rhs, cols, leaf_tr, inner_tr)))


def sides_kernel(own, mate, after, out, sems):
    del after
    wide = out.shape[1] // 2
    core = lax.rem(lax.axis_index("rhs"), 2)
    start = pl.multiple_of((1 - core) * (own.shape[1] - wide), wide)
    pairs = [
        (ref.at[:, pl.ds(start, wide)], out.at[:, pl.ds(at * wide, wide)])
        for at, ref in enumerate((own, mate))
    ]
    for copy in fetched(pairs, sems):
        copy.wait()


def run_sides(own, mate, wide, after):
    return pl.pallas_call(
        sides_kernel,
        in_specs=[ANY] * 3,
        out_specs=VMEM,
        out_shape=pltpu.VMEM((own.shape[0], 2 * wide), own.dtype),
        scratch_shapes=[pltpu.SemaphoreType.DMA((2,))],
        compiler_params=limit(1),
        cost_estimate=pl.CostEstimate(flops=0, bytes_accessed=400_000, transcendentals=0),
        name="sides",
    )(in_hbm(own), mate, after)


def join_kernel(*refs):
    parts, (after, out, sems) = refs[:-3], refs[-3:]
    del after
    pairs = []
    column = 0
    for part in parts:
        width = part.shape[1]
        pairs.append((part, out.at[:, pl.ds(column, width)]))
        column += width
    for copy in fetched(pairs, sems):
        copy.wait()


def run_join(parts, after):
    rows = parts[0].shape[0]
    width = sum(part.shape[1] for part in parts)
    return pl.pallas_call(
        join_kernel,
        in_specs=[ANY] * (len(parts) + 1),
        out_specs=VMEM,
        out_shape=pltpu.VMEM((rows, width), parts[0].dtype),
        scratch_shapes=[pltpu.SemaphoreType.DMA((len(parts),))],
        compiler_params=limit(1),
        cost_estimate=pl.CostEstimate(flops=0, bytes_accessed=1_000_000, transcendentals=0),
        name="join",
    )(*parts, after)


def chosen(table_hbm, table, wanted, picked, sems):
    skel, _, nodes = table.shape
    lane = lax.broadcasted_iota(jnp.int32, (16, nodes), 1)
    select = (wanted == lane).astype(BF16)
    chunk = 8
    copies = fetched(
        [
            (table_hbm.at[pl.ds(at, chunk)], table.at[pl.ds(at, chunk)])
            for at in range(0, skel, chunk)
        ],
        sems,
    )

    def finish():
        dot = functools.partial(
            lax.dot_general, select, dimension_numbers=TURNED, preferred_element_type=F32
        )
        group = 4
        for k in range(0, skel, group):
            if k % chunk == 0:
                copies[k // chunk].wait()
            top, low = halves(table[k : k + group].reshape(group * skel, nodes))
            rows = dot(top) + dot(low)
            for at in range(group):
                picked[pl.ds(16 * (k + at), 16), :] = rows[:, at * skel : (at + 1) * skel]

    return finish


def node_rows(nodes):
    return lax.broadcasted_iota(jnp.int32, (16, nodes), 0)


def pick_kernel(depth, tree_hbm, after, out, tree, picked, sems):
    del after
    skel, _, nodes = tree.shape
    heap = lax.axis_size("leaf") + lax.axis_index("leaf")
    row = node_rows(nodes)
    wanted = (lax.shift_right_logical(heap, row >> 1) ^ (row & 1)) - 2
    chosen(tree_hbm, tree, wanted, picked, sems)()
    for bit in range(depth - 1):
        for side in range(2):
            out[bit, side * skel : (side + 1) * skel, :] = picked[
                pl.ds(2 * bit + side, skel, stride=16), :
            ]


def run_pick(depth, tree_tr, after):
    skel = tree_tr.shape[0]
    return pl.pallas_call(
        functools.partial(pick_kernel, depth),
        in_specs=[ANY] * 2,
        out_specs=VMEM,
        out_shape=pltpu.VMEM((depth - 1, 2 * skel, skel), F32),
        scratch_shapes=[
            pltpu.VMEM(tree_tr.shape, F32),
            pltpu.VMEM((16 * skel, skel), F32),
            pltpu.SemaphoreType.DMA((skel // 8,)),
        ],
        compiler_params=limit(6),
        cost_estimate=pl.CostEstimate(flops=200_000_000, bytes_accessed=2_000_000, transcendentals=0),
        name="pick",
    )(in_hbm(tree_tr), after)


def lift_kernel(bit, current, other, mats, *rest):
    out = rest[-1]
    out[...] = dot3(jnp.concatenate([current[...], other[...]], axis=1), mats[bit])


def run_lift(bit, current, other, mats, after):
    return pl.pallas_call(
        functools.partial(lift_kernel, bit),
        in_specs=[VMEM] * 3 + [ANY] * len(after),
        out_specs=VMEM,
        out_shape=pltpu.VMEM(current.shape, F32),
        compiler_params=limit(1),
        cost_estimate=pl.CostEstimate(flops=2_000_000, bytes_accessed=100_000, transcendentals=0),
        name="lift",
    )(current, other, mats, *after)


def prep_kernel(
    coeffs,
    second,
    first,
    after,
    leaf_tr_hbm,
    leaf_cp_hbm,
    inner_tr_hbm,
    inner_cp_hbm,
    local_ref,
    reach_ref,
    leaf_tr,
    leaf_cp,
    inner_tr,
    inner_cp,
    sems,
):
    del after
    copies = fetched(
        [
            (inner_cp_hbm, inner_cp),
            (inner_tr_hbm, inner_tr),
            (leaf_cp_hbm, leaf_cp),
            (leaf_tr_hbm, leaf_tr),
        ],
        sems,
    )

    def coupled(values, table):
        a = dot3(values[:, 64:], table[:64], TURNED)
        b = dot3(values[:, :64], table[64:], TURNED)
        return jnp.concatenate([a, b], axis=1)

    for copy in copies:
        copy.wait()
    tops = coupled(first[...], inner_cp[0])
    mids = []
    for side in range(2):
        own = coupled(second[:, side * 128 : (side + 1) * 128], inner_cp[1 + side])
        mids.append(own + dot3(tops[:, side * 64 : (side + 1) * 64], inner_tr[1 + side], TURNED))
    reach_top = inner_tr[0]
    for pair in range(4):
        side = pair // 2
        low = (pair % 2) * 64
        own = coupled(coeffs[:, pair * 128 : (pair + 1) * 128], leaf_cp[pair])
        own = own + dot3(mids[side][:, low : low + 64], leaf_tr[pair], TURNED)
        local_ref[:, pair * 128 : (pair + 1) * 128] = own
        if pair % 2 == 0:
            reach_mid = dot3(inner_tr[1 + side], reach_top[side * 64 : (side + 1) * 64])
        reach_ref[pair * 128 : (pair + 1) * 128, :] = dot3(leaf_tr[pair], reach_mid[low : low + 64])


def run_prep(coeffs, second, first, leaf_tr, leaf_cp, inner_tr, inner_cp, after):
    rows = coeffs.shape[0]
    skel = first.shape[1] // 2
    tables = (leaf_tr, leaf_cp, inner_tr, inner_cp)
    return pl.pallas_call(
        prep_kernel,
        in_specs=[VMEM] * 3 + [ANY] * 5,
        out_specs=[VMEM] * 2,
        out_shape=[pltpu.VMEM((rows, 8 * skel), F32), pltpu.VMEM((8 * skel, skel), F32)],
        scratch_shapes=[pltpu.VMEM(x.shape, F32) for x in tables] + [pltpu.SemaphoreType.DMA((4,))],
        compiler_params=limit(4),
        cost_estimate=pl.CostEstimate(flops=200_000_000, bytes_accessed=1_000_000, transcendentals=0),
        name="prep",
    )(coeffs, second, first, after, *map(in_hbm, tables))


def turn_kernel(depth, mats, after, tree_hbm, out, tree, picked, sems):
    del after
    skel, _, nodes = tree.shape
    heap = lax.axis_size("leaf") + lax.axis_index("leaf")
    wanted = lax.shift_right_logical(heap, node_rows(nodes)) - 2
    finish = chosen(tree_hbm, tree, wanted, picked, sems)
    chains = [mats[0, :skel]]
    for bit in range(1, depth - 1):
        chains.append(dot3(chains[-1], mats[bit, :skel]))
    finish()
    for bit in range(depth):
        couple = picked[pl.ds(bit, skel, stride=16), :]
        out[bit] = dot3(chains[bit - 1], couple) if bit else couple


def run_turn(depth, mats, tree_cp, after):
    skel = tree_cp.shape[0]
    return pl.pallas_call(
        functools.partial(turn_kernel, depth),
        in_specs=[VMEM] + [ANY] * 2,
        out_specs=VMEM,
        out_shape=pltpu.VMEM((depth, skel, skel), F32),
        scratch_shapes=[
            pltpu.VMEM(tree_cp.shape, F32),
            pltpu.VMEM((16 * skel, skel), F32),
            pltpu.SemaphoreType.DMA((skel // 8,)),
        ],
        compiler_params=limit(6),
        cost_estimate=pl.CostEstimate(flops=200_000_000, bytes_accessed=2_000_000, transcendentals=0),
        name="turn",
    )(mats, after, in_hbm(tree_cp))


def near_kernel(index, own, mate, far, edge, edge_far, relay, diag, near, after, *rest):
    del after
    kept, beside, across, grid = rest
    rows, width = own.shape
    count, part, size = diag.shape
    wide = 2 * size
    core = lax.rem(lax.axis_index("rhs"), 2)
    here = pl.multiple_of(core * (width + wide), wide)
    there = pl.multiple_of((1 - core) * (width + wide), wide)

    def place(source, start, length, group, column):
        target = (pl.ds(group * rows, rows), pl.ds(column, length))
        grid[target] = source[:, start : start + length]

    place(own, 0, width, 0, wide)
    place(mate, 0, width, 1, wide)
    place(far, 0, width, 2, wide)
    place(relay, 0, width, 3, wide)
    place(edge, 0, wide, 0, here)
    place(edge, wide, wide, 1, here)
    place(edge_far, 0, wide, 2, here)
    place(edge_far, wide, wide, 3, here)
    place(relay, width, wide, 1, there)
    place(relay, width + wide, wide, 0, there)
    place(relay, width + 2 * wide, wide, 3, there)
    place(relay, width + 3 * wide, wide, 2, there)
    base = lax.axis_index("leaf") * count - 2
    dot = functools.partial(
        lax.dot_general, dimension_numbers=TURNED, preferred_element_type=F32
    )
    for leaf in range(count):
        total = dot(grid[:, (leaf + 2) * size : (leaf + 3) * size], diag[leaf])
        for j in range(near.shape[1]):
            column = pl.multiple_of((index[j, leaf] - base) * size, size)
            total = total + dot(grid[:, pl.ds(column, size)], near[leaf, j])
        here = slice(leaf * part, (leaf + 1) * part)
        kept[:, here] = total[:rows]
        beside[:, here] = total[rows : 2 * rows].astype(BF16)
        across[:, here] = total[2 * rows : 3 * rows].astype(BF16)
        here = slice((count + leaf) * part, (count + leaf + 1) * part)
        across[:, here] = total[3 * rows :].astype(BF16)


def run_near(index, own, mate, far, edge, edge_far, relay, diag, near, after):
    rows, width = own.shape
    count, part, size = diag.shape
    return pl.pallas_call(
        near_kernel,
        in_specs=[pl.BlockSpec(memory_space=pltpu.SMEM)] + [VMEM] * 8 + [ANY],
        out_specs=[VMEM] * 3,
        out_shape=[
            pltpu.VMEM((rows, count * part), F32),
            pltpu.VMEM((rows, count * part), BF16),
            pltpu.VMEM((rows, 2 * count * part), BF16),
        ],
        scratch_shapes=[pltpu.VMEM((4 * rows, width + 4 * size), BF16)],
        compiler_params=limit(12),
        cost_estimate=pl.CostEstimate(flops=800_000_000, bytes_accessed=6_000_000, transcendentals=0),
        name="near",
    )(index, own, mate, far, edge, edge_far, relay, diag, near, after)


def last_kernel(*refs):
    others, (turn, reach, local, basis, kept, across, beside, out) = refs[:-8], refs[-8:]
    rows = local.shape[0]
    skel = turn.shape[1]
    count = local.shape[1] // skel
    size = basis.shape[1] // count
    part = kept.shape[1] // count
    half = count * part
    total = None
    for bit, other in enumerate(others):
        term = dot3(other[...], turn[bit], TURNED)
        total = term if total is None else total + term
    leaf = (local[...] + dot3(total, reach[...], TURNED)).astype(BF16)
    place = lax.axis_index("rhs")
    for at in range(count):
        span = slice(at * size, (at + 1) * size)
        out[:, span] = lax.dot_general(
            leaf[:, at * skel : (at + 1) * skel], basis[:, span], PLAIN, preferred_element_type=F32
        )
        for group, (close, start) in enumerate(((kept, 0), (beside, 0), (across, 0), (beside, half))):
            column = pl.multiple_of(at * size + (place ^ group) * part, part)
            here = pl.ds(column, part)
            start += at * part
            out[:, here] = out[:, here] + close[:, start : start + part].astype(F32)


def run_last(others, turn, reach, local, basis, kept, across, beside):
    rows = local.shape[0]
    return pl.pallas_call(
        last_kernel,
        in_specs=[VMEM] * (len(others) + 7),
        out_specs=VMEM,
        out_shape=jax.ShapeDtypeStruct((rows, basis.shape[1]), F32),
        compiler_params=limit(6),
        cost_estimate=pl.CostEstimate(flops=200_000_000, bytes_accessed=2_000_000, transcendentals=0),
        name="last",
    )(*others, turn, reach, local, basis, kept, across, beside)


def local(
    rhs_block,
    col_basis,
    row_basis,
    leaf_transfer,
    leaf_coupling,
    inner_transfer,
    inner_coupling,
    tree_transfer,
    tree_coupling,
    diag_blocks,
    near_blocks,
    near_leaves,
):
    width = rhs_block.shape[1]
    count = leaf_transfer.shape[0]
    wide = 2 * (width // count)
    skel = col_basis.shape[0]
    span = lax.axis_size("leaf")
    ranks = lax.axis_size("rhs")
    depth = span.bit_length() - 1
    leaf_tr = leaf_transfer.reshape(count // 2, 2 * skel, skel)
    leaf_cp = leaf_coupling.reshape(count // 2, 2 * skel, skel)
    inner_tr = inner_transfer.reshape(count // 2 - 1, 2 * skel, skel)
    inner_cp = inner_coupling.reshape(count // 2 - 1, 2 * skel, skel)

    mate = swapped(rhs_block, "rhs", 1)
    far = swapped(rhs_block, "rhs", 2)

    coeffs, second, first, block = run_up(rhs_block, col_basis, leaf_tr, inner_tr)
    mats = run_pick(depth, jnp.transpose(tree_transfer, (1, 2, 0)), block)
    sides = run_sides(rhs_block, mate, wide, block)
    same, across = [], []
    for i in range(span):
        for q in range(ranks):
            to = i + 1 if q % 2 == 0 else i - 1
            if 0 <= to < span:
                same.append((i * ranks + q, to * ranks + q))
                across.append((i * ranks + q, to * ranks + (q ^ 2)))
    edge = lax.ppermute(sides, ("leaf", "rhs"), same)
    edge_far = lax.ppermute(sides, ("leaf", "rhs"), across)

    others = []

    def step(current, beside):
        bit = len(others)
        others.append(swapped(current, "leaf", 1 << bit))
        return run_lift(bit, current, others[-1], mats, beside)

    current = step(block, [sides])
    local_part, reach = run_prep(
        coeffs, second, first, leaf_tr, leaf_cp, inner_tr, inner_cp, current
    )
    current = step(current, [reach])
    joined = run_join([far, edge, edge_far], current)
    relay = swapped(joined, "rhs", 1)
    current = step(current, [joined])
    kept, beside, passed = run_near(
        near_leaves.T, rhs_block, mate, far, edge, edge_far, relay, diag_blocks, near_blocks, current
    )
    passed = swapped(passed, "rhs", 2)
    current = step(current, [kept])
    turn = run_turn(depth, mats, jnp.transpose(tree_coupling, (1, 2, 0)), current)
    half = passed.shape[1] // 2
    joined = run_join([beside, passed[:, half:]], current)
    beside = swapped(joined, "rhs", 1)
    current = step(current, [turn, joined])
    others.append(swapped(current, "leaf", 1 << len(others)))
    return run_last(others, turn, reach, local_part, row_basis, kept, passed, beside)


def solution(mesh):
    in_specs = (
        P("rhs", "leaf"),
        P(None, "leaf"),
        P(None, "leaf"),
        P("leaf", None, None),
        P("leaf", None, None),
        P("leaf", None, None, None),
        P("leaf", None, None, None),
        P(),
        P(),
        P("leaf", "rhs", None),
        P("leaf", None, "rhs", None),
        P("leaf", None),
    )
    out_specs = P("rhs", "leaf")
    return jax.shard_map(local, mesh=mesh, in_specs=in_specs, out_specs=out_specs, check_vma=False)
```

```python
import functools

import jax
import jax.numpy as jnp
from jax import lax
from jax.experimental import pallas as pl
from jax.experimental.pallas import tpu as pltpu
from jax.sharding import PartitionSpec as P

HIGH = lax.Precision.HIGHEST
F32 = jnp.float32
BF16 = jnp.bfloat16
VMEM = pl.BlockSpec(memory_space=pltpu.VMEM)
ANY = pl.BlockSpec(memory_space=pl.ANY)
LIGHT = pl.CostEstimate(flops=0, bytes_accessed=0, transcendentals=0)
HEAVY = pl.CostEstimate(flops=20_000_000_000, bytes_accessed=60_000_000, transcendentals=0)
MIDDLE = pl.CostEstimate(flops=0, bytes_accessed=11_000_000, transcendentals=0)
PLAIN = (((1,), (0,)), ((), ()))
TURNED = (((1,), (1,)), ((), ()))


def halves(x):
    top = x.astype(BF16)
    return top, (x - top.astype(F32)).astype(BF16)


def dot3(a, b, dims=PLAIN):
    ah, al = halves(a)
    bh, bl = halves(b)
    dot = functools.partial(lax.dot_general, dimension_numbers=dims, preferred_element_type=F32)
    return dot(ah, bh) + (dot(ah, bl) + dot(al, bh))


def swapped(x, axis, bit):
    count = lax.axis_size(axis)
    return lax.ppermute(x, axis, [(i, i ^ bit) for i in range(count)])


def limit(mib):
    return pltpu.CompilerParams(vmem_limit_bytes=mib << 20)


def in_hbm(x):
    return pltpu.with_memory_space_constraint(x, pltpu.HBM)


def fetched(pairs, sems):
    copies = []
    for at, (source, target) in enumerate(pairs):
        copy = pltpu.make_async_copy(source, target, sems.at[at])
        copy.start()
        copies.append(copy)
    return copies


def up_kernel(
    rhs_hbm,
    cols_hbm,
    leaf_hbm,
    inner_hbm,
    tree_hbm,
    rhs,
    tree,
    coeffs,
    second,
    first,
    block,
    packet,
    outward,
    cols,
    leaf_tr,
    inner_tr,
    sems,
):
    half = rhs.shape[1] // 2
    size = rhs.shape[1] // 8
    wide = 2 * size
    pairs = []
    for side in range(2):
        span = pl.ds(side * half, half)
        pairs += [(rhs_hbm.at[:, span], rhs.at[:, span]), (cols_hbm.at[:, span], cols.at[:, span])]
    pairs += [(leaf_hbm, leaf_tr), (inner_hbm, inner_tr), (tree_hbm, tree)]
    copies = fetched(pairs, sems)
    parts = []
    for leaf in range(8):
        if leaf % 4 == 0:
            copies[leaf // 2].wait()
            copies[leaf // 2 + 1].wait()
        span = slice(leaf * size, (leaf + 1) * size)
        parts.append(
            lax.dot_general(rhs[:, span], cols[:, span], TURNED, preferred_element_type=F32)
        )
    copies[4].wait()
    copies[5].wait()
    ups = []
    for pair in range(4):
        both = jnp.concatenate(parts[2 * pair : 2 * pair + 2], axis=1)
        coeffs[:, pair * 128 : (pair + 1) * 128] = both
        ups.append(dot3(both, leaf_tr[pair]))
    left = jnp.concatenate(ups[:2], axis=1)
    right = jnp.concatenate(ups[2:], axis=1)
    second[:, :128] = left
    second[:, 128:] = right
    both = jnp.concatenate([dot3(left, inner_tr[1]), dot3(right, inner_tr[2])], axis=1)
    first[...] = both
    total = dot3(both, inner_tr[0])
    block[...] = total
    packet[:, :128] = jnp.concatenate(halves(total), axis=1)
    odd = lax.rem(lax.axis_index("leaf"), 2)
    inner_side = pl.multiple_of((1 - odd) * (rhs.shape[1] - wide), wide)
    outer_side = pl.multiple_of(odd * (rhs.shape[1] - wide), wide)
    packet[:, 128:] = rhs[:, pl.ds(inner_side, wide)]
    outward[...] = rhs[:, pl.ds(outer_side, wide)]
    copies[6].wait()


def run_up(rhs, cols, leaf_tr, inner_tr, tree_tr):
    rows, width = rhs.shape
    skel = cols.shape[0]
    wide = width // 4
    tables = (cols, leaf_tr, inner_tr)
    return pl.pallas_call(
        up_kernel,
        in_specs=[ANY] * 5,
        out_specs=[VMEM] * 8,
        out_shape=[
            pltpu.VMEM(rhs.shape, rhs.dtype),
            pltpu.VMEM(tree_tr.shape, F32),
            pltpu.VMEM((rows, 8 * skel), F32),
            pltpu.VMEM((rows, 4 * skel), F32),
            pltpu.VMEM((rows, 2 * skel), F32),
            pltpu.VMEM((rows, skel), F32),
            pltpu.VMEM((rows, 2 * skel + wide), BF16),
            pltpu.VMEM((rows, wide), BF16),
        ],
        scratch_shapes=[pltpu.VMEM(x.shape, x.dtype) for x in tables]
        + [pltpu.SemaphoreType.DMA((7,))],
        compiler_params=limit(8),
        cost_estimate=LIGHT,
        name="up",
    )(*map(in_hbm, (rhs, cols, leaf_tr, inner_tr, tree_tr)))


def join_kernel(spans, *refs):
    refs, (out, sems) = refs[:-2], refs[-2:]
    pairs = []
    column = 0
    for part, (start, width) in zip(refs, spans):
        pairs.append((part.at[:, pl.ds(start, width)], out.at[:, pl.ds(column, width)]))
        column += width
    for copy in fetched(pairs, sems):
        copy.wait()


def run_join(parts, after=()):
    spans = [part[1:] for part in parts]
    arrays = [part[0] for part in parts]
    return pl.pallas_call(
        functools.partial(join_kernel, spans),
        in_specs=[ANY] * (len(parts) + len(after)),
        out_specs=VMEM,
        out_shape=pltpu.VMEM((arrays[0].shape[0], sum(w for _, w in spans)), arrays[0].dtype),
        scratch_shapes=[pltpu.SemaphoreType.DMA((len(parts),))],
        compiler_params=limit(1),
        cost_estimate=LIGHT,
        name="join",
    )(*arrays, *after)


def choose(table, wanted, picked):
    skel, _, nodes = table.shape
    select = (wanted == lax.broadcasted_iota(jnp.int32, (16, nodes), 1)).astype(BF16)
    dot = functools.partial(
        lax.dot_general, select, dimension_numbers=TURNED, preferred_element_type=F32
    )
    group = 4
    for k in range(0, skel, group):
        top, low = halves(table[k : k + group].reshape(group * skel, nodes))
        rows = dot(top) + dot(low)
        for at in range(group):
            picked[pl.ds(16 * (k + at), 16), :] = rows[:, at * skel : (at + 1) * skel]


def node_rows(nodes):
    return lax.broadcasted_iota(jnp.int32, (16, nodes), 0)


def pick_kernel(depth, tree, out, picked):
    skel, _, nodes = tree.shape
    heap = lax.axis_size("leaf") + lax.axis_index("leaf")
    row = node_rows(nodes)
    choose(tree, (lax.shift_right_logical(heap, row >> 1) ^ (row & 1)) - 2, picked)
    for bit in range(depth - 1):
        for side in range(2):
            out[bit, side * skel : (side + 1) * skel, :] = picked[
                pl.ds(2 * bit + side, skel, stride=16), :
            ]


def run_pick(depth, tree):
    skel = tree.shape[0]
    return pl.pallas_call(
        functools.partial(pick_kernel, depth),
        in_specs=[VMEM],
        out_specs=VMEM,
        out_shape=pltpu.VMEM((depth - 1, 2 * skel, skel), F32),
        scratch_shapes=[pltpu.VMEM((16 * skel, skel), F32)],
        compiler_params=limit(6),
        cost_estimate=LIGHT,
        name="pick",
    )(tree)


def first_lift_kernel(current, packet, mats, *rest):
    out, other = rest[-2:]
    skel = current.shape[1]
    sibling = packet[:, :skel].astype(F32) + packet[:, skel : 2 * skel].astype(F32)
    other[...] = sibling
    out[...] = dot3(jnp.concatenate([current[...], sibling], axis=1), mats[0])


def run_first_lift(current, packet, mats, after):
    return pl.pallas_call(
        first_lift_kernel,
        in_specs=[VMEM] * 3 + [ANY] * len(after),
        out_specs=[VMEM] * 2,
        out_shape=[pltpu.VMEM(current.shape, F32)] * 2,
        compiler_params=limit(1),
        cost_estimate=HEAVY,
        name="lift",
    )(current, packet, mats, *after)


def lift_kernel(bit, current, other, mats, *rest):
    out = rest[-1]
    skel = mats.shape[-1]
    both = jnp.concatenate([current[:, :skel], other[:, :skel]], axis=1)
    if out.shape[1] > skel:
        out[...] = jnp.zeros_like(out)
    out[:, :skel] = dot3(both, mats[bit])


def run_lift(bit, current, other, mats, after, width):
    return pl.pallas_call(
        functools.partial(lift_kernel, bit),
        in_specs=[VMEM] * 3 + [ANY] * len(after),
        out_specs=VMEM,
        out_shape=pltpu.VMEM((current.shape[0], width), F32),
        compiler_params=limit(1),
        cost_estimate=(HEAVY, LIGHT, MIDDLE, HEAVY, HEAVY)[bit],
        name="lift",
    )(current, other, mats, *after)


def prep_kernel(
    coeffs,
    second,
    first,
    after,
    leaf_tr_hbm,
    leaf_cp_hbm,
    inner_tr_hbm,
    inner_cp_hbm,
    tree_hbm,
    local_ref,
    reach_ref,
    tree,
    leaf_tr,
    leaf_cp,
    inner_tr,
    inner_cp,
    sems,
):
    del after
    copies = fetched(
        [
            (inner_cp_hbm, inner_cp),
            (inner_tr_hbm, inner_tr),
            (leaf_cp_hbm, leaf_cp),
            (leaf_tr_hbm, leaf_tr),
            (tree_hbm, tree),
        ],
        sems,
    )

    def coupled(values, table):
        a = dot3(values[:, 64:], table[:64], TURNED)
        b = dot3(values[:, :64], table[64:], TURNED)
        return jnp.concatenate([a, b], axis=1)

    for copy in copies[:4]:
        copy.wait()
    tops = coupled(first[...], inner_cp[0])
    mids = []
    for side in range(2):
        own = coupled(second[:, side * 128 : (side + 1) * 128], inner_cp[1 + side])
        mids.append(own + dot3(tops[:, side * 64 : (side + 1) * 64], inner_tr[1 + side], TURNED))
    reach_top = inner_tr[0]
    for pair in range(4):
        side = pair // 2
        low = (pair % 2) * 64
        own = coupled(coeffs[:, pair * 128 : (pair + 1) * 128], leaf_cp[pair])
        own = own + dot3(mids[side][:, low : low + 64], leaf_tr[pair], TURNED)
        local_ref[:, pair * 128 : (pair + 1) * 128] = own
        if pair % 2 == 0:
            reach_mid = dot3(inner_tr[1 + side], reach_top[side * 64 : (side + 1) * 64])
        reach_ref[pair * 128 : (pair + 1) * 128, :] = dot3(leaf_tr[pair], reach_mid[low : low + 64])
    copies[4].wait()


def run_prep(coeffs, second, first, leaf_tr, leaf_cp, inner_tr, inner_cp, tree_cp, after):
    rows = coeffs.shape[0]
    skel = first.shape[1] // 2
    tables = (leaf_tr, leaf_cp, inner_tr, inner_cp)
    return pl.pallas_call(
        prep_kernel,
        in_specs=[VMEM] * 3 + [ANY] * 6,
        out_specs=[VMEM] * 3,
        out_shape=[
            pltpu.VMEM((rows, 8 * skel), F32),
            pltpu.VMEM((8 * skel, skel), F32),
            pltpu.VMEM(tree_cp.shape, F32),
        ],
        scratch_shapes=[pltpu.VMEM(x.shape, F32) for x in tables] + [pltpu.SemaphoreType.DMA((5,))],
        compiler_params=limit(6),
        cost_estimate=LIGHT,
        name="prep",
    )(coeffs, second, first, after, *map(in_hbm, (*tables, tree_cp)))


def turn_kernel(depth, mats, tree, after, out, picked):
    del after
    skel, _, nodes = tree.shape
    heap = lax.axis_size("leaf") + lax.axis_index("leaf")
    choose(tree, lax.shift_right_logical(heap, node_rows(nodes)) - 2, picked)
    chain = None
    for bit in range(depth):
        couple = picked[pl.ds(bit, skel, stride=16), :]
        out[bit] = couple if chain is None else dot3(chain, couple)
        if bit + 1 < depth:
            step = mats[bit, :skel]
            chain = step if chain is None else dot3(chain, step)


def run_turn(depth, mats, tree, after):
    skel = tree.shape[0]
    return pl.pallas_call(
        functools.partial(turn_kernel, depth),
        in_specs=[VMEM] * 2 + [ANY],
        out_specs=VMEM,
        out_shape=pltpu.VMEM((depth, skel, skel), F32),
        scratch_shapes=[pltpu.VMEM((16 * skel, skel), F32)],
        compiler_params=limit(6),
        cost_estimate=LIGHT,
        name="turn",
    )(mats, tree, after)


def near_kernel(index, own, far, edge, edge_far, relay, diag, near, after, *rest):
    del after
    outs, grid = rest[:4], rest[4]
    rows, width = own.shape
    count, part, size = diag.shape
    wide = 2 * size
    odd = lax.rem(lax.axis_index("leaf"), 2)
    inner = pl.multiple_of((1 - odd) * (width + wide), wide)
    outer = pl.multiple_of(odd * (width + wide), wide)

    def place(source, start, length, group, column):
        target = (pl.ds(group * rows, rows), pl.ds(column, length))
        grid[target] = source[:, start : start + length]

    place(own, 0, width, 0, wide)
    place(relay, 0, width, 1, wide)
    place(far, 0, width, 2, wide)
    place(relay, width, width, 3, wide)
    for group, (source, start) in enumerate(
        ((edge, 0), (relay, 2 * width), (edge_far, 0), (relay, 2 * width + 2 * wide))
    ):
        place(source, start, wide, group, inner)
        place(source, start + wide, wide, group, outer)
    base = lax.axis_index("leaf") * count - 2
    dot = functools.partial(
        lax.dot_general, dimension_numbers=TURNED, preferred_element_type=F32
    )
    for leaf in range(count):
        total = dot(grid[:, (leaf + 2) * size : (leaf + 3) * size], diag[leaf])
        for j in range(near.shape[1]):
            column = pl.multiple_of((index[j, leaf] - base) * size, size)
            total = total + dot(grid[:, pl.ds(column, size)], near[leaf, j])
        for group, out in enumerate(outs):
            block = total[group * rows : (group + 1) * rows]
            out[:, leaf * part : (leaf + 1) * part] = block.astype(out.dtype)


def run_near(index, own, far, edge, edge_far, relay, diag, near, after):
    rows, width = own.shape
    count, part, size = diag.shape
    return pl.pallas_call(
        near_kernel,
        in_specs=[pl.BlockSpec(memory_space=pltpu.SMEM)] + [VMEM] * 7 + [ANY],
        out_specs=[VMEM] * 4,
        out_shape=[pltpu.VMEM((rows, count * part), F32)]
        + [pltpu.VMEM((rows, count * part), BF16)] * 3,
        scratch_shapes=[pltpu.VMEM((4 * rows, width + 4 * size), BF16)],
        compiler_params=limit(12),
        cost_estimate=LIGHT,
        name="near",
    )(index, own, far, edge, edge_far, relay, diag, near, after)


def settle_kernel(*refs):
    others, (turn, reach, local, leaf, final) = refs[:-5], refs[-5:]
    skel = turn.shape[1]
    total = None
    for bit, other in enumerate(others):
        term = dot3(other[:, :skel], turn[bit], TURNED)
        total = term if total is None else total + term
    leaf[...] = local[...] + dot3(total, reach[...], TURNED)
    final[...] = dot3(reach[...], turn[len(others)])


def run_settle(others, turn, reach, local):
    return pl.pallas_call(
        settle_kernel,
        in_specs=[VMEM] * (len(others) + 3),
        out_specs=[VMEM] * 2,
        out_shape=[pltpu.VMEM(local.shape, F32), pltpu.VMEM(reach.shape, F32)],
        compiler_params=limit(2),
        cost_estimate=LIGHT,
        name="settle",
    )(*others, turn, reach, local)


def last_kernel(other, final, local, basis, *rest):
    close, out = rest[:-1], rest[-1]
    skel = other.shape[1]
    count = local.shape[1] // skel
    size = basis.shape[1] // count
    part = close[0].shape[1] // count
    leaf = (local[...] + dot3(other[...], final[...], TURNED)).astype(BF16)
    place = lax.axis_index("rhs")
    for at in range(count):
        span = slice(at * size, (at + 1) * size)
        out[:, span] = lax.dot_general(
            leaf[:, at * skel : (at + 1) * skel], basis[:, span], PLAIN, preferred_element_type=F32
        )
        for group, block in enumerate(close):
            column = pl.multiple_of(at * size + (place ^ group) * part, part)
            here = pl.ds(column, part)
            out[:, here] = out[:, here] + block[:, at * part : (at + 1) * part].astype(F32)


def run_last(other, final, local, basis, close):
    rows = local.shape[0]
    return pl.pallas_call(
        last_kernel,
        in_specs=[VMEM] * (len(close) + 4),
        out_specs=VMEM,
        out_shape=jax.ShapeDtypeStruct((rows, basis.shape[1]), F32),
        compiler_params=limit(6),
        cost_estimate=LIGHT,
        name="last",
    )(other, final, local, basis, *close)


def local(
    rhs_block,
    col_basis,
    row_basis,
    leaf_transfer,
    leaf_coupling,
    inner_transfer,
    inner_coupling,
    tree_transfer,
    tree_coupling,
    diag_blocks,
    near_blocks,
    near_leaves,
):
    width = rhs_block.shape[1]
    count = leaf_transfer.shape[0]
    wide = 2 * (width // count)
    skel = col_basis.shape[0]
    span = lax.axis_size("leaf")
    ranks = lax.axis_size("rhs")
    depth = span.bit_length() - 1
    leaf_tr = leaf_transfer.reshape(count // 2, 2 * skel, skel)
    leaf_cp = leaf_coupling.reshape(count // 2, 2 * skel, skel)
    inner_tr = inner_transfer.reshape(count // 2 - 1, 2 * skel, skel)
    inner_cp = inner_coupling.reshape(count // 2 - 1, 2 * skel, skel)

    far = swapped(rhs_block, "rhs", 2)
    own, tree, coeffs, second, first, block, packet, outward = run_up(
        rhs_block, col_basis, leaf_tr, inner_tr, jnp.transpose(tree_transfer, (1, 2, 0))
    )

    packet = swapped(packet, "leaf", 1)
    mats = run_pick(depth, tree)
    pairs = [(i, i + 1) for i in range(1, span - 1, 2)]
    outward = lax.ppermute(outward, "leaf", pairs + [(j, i) for i, j in pairs])
    current, other = run_first_lift(block, packet, mats, [])
    others = [other]

    def step(current, beside, width=skel):
        bit = len(others)
        others.append(swapped(current, "leaf", 1 << bit))
        return run_lift(bit, current, others[-1], mats, beside, width)

    local_part, reach, tree = run_prep(
        coeffs,
        second,
        first,
        leaf_tr,
        leaf_cp,
        inner_tr,
        inner_cp,
        jnp.transpose(tree_coupling, (1, 2, 0)),
        current,
    )
    current = step(current, [reach])
    turn = run_turn(depth, mats, tree, current)
    edge = run_join([(packet, 2 * skel, wide), (outward, 0, wide)], [current])
    edge_far = swapped(edge, "rhs", 2)
    current = step(current, [turn])
    joined = run_join(
        [(own, 0, width), (far, 0, width), (edge, 0, 2 * wide), (edge_far, 0, 2 * wide)], [current]
    )
    relay = swapped(joined, "rhs", 1)
    current = step(current, [joined])
    close = run_near(
        near_leaves.T, own, far, edge, edge_far, relay, diag_blocks, near_blocks, current
    )
    current = step(current, close[:1])
    close = [close[0]] + [swapped(close[k], "rhs", k) for k in range(1, ranks)]
    leaf_part, final = run_settle(others, turn, reach, local_part)
    other = swapped(current, "leaf", 1 << len(others))
    return run_last(other, final, leaf_part, row_basis, close)


def solution(mesh):
    in_specs = (
        P("rhs", "leaf"),
        P(None, "leaf"),
        P(None, "leaf"),
        P("leaf", None, None),
        P("leaf", None, None),
        P("leaf", None, None, None),
        P("leaf", None, None, None),
        P(),
        P(),
        P("leaf", "rhs", None),
        P("leaf", None, "rhs", None),
        P("leaf", None),
    )
    out_specs = P("rhs", "leaf")
    return jax.shard_map(local, mesh=mesh, in_specs=in_specs, out_specs=out_specs, check_vma=False)
```

```python
import functools

import jax
import jax.numpy as jnp
from jax import lax
from jax.experimental import pallas as pl
from jax.experimental.pallas import tpu as pltpu
from jax.sharding import PartitionSpec as P

F32 = jnp.float32
BF16 = jnp.bfloat16
VMEM = pl.BlockSpec(memory_space=pltpu.VMEM)
ANY = pl.BlockSpec(memory_space=pl.ANY)
PLAIN = (((1,), (0,)), ((), ()))
TURNED = (((1,), (1,)), ((), ()))


def work(flops):
    return pl.CostEstimate(flops=flops, bytes_accessed=0, transcendentals=0)


LIFT_WORK = (20_000_000_000, 500_000_000, 2_500_000_000, 20_000_000_000, 20_000_000_000)
LIGHT = work(0)


def halves(x):
    top = x.astype(BF16)
    return top, (x - top.astype(F32)).astype(BF16)


def dot3(a, b, dims=PLAIN):
    ah, al = halves(a)
    bh, bl = halves(b)
    dot = functools.partial(lax.dot_general, dimension_numbers=dims, preferred_element_type=F32)
    return dot(ah, bh) + (dot(ah, bl) + dot(al, bh))


def swapped(x, axis, bit):
    count = lax.axis_size(axis)
    return lax.ppermute(x, axis, [(i, i ^ bit) for i in range(count)])


def limit(mib):
    return pltpu.CompilerParams(vmem_limit_bytes=mib << 20)


def in_hbm(x):
    return pltpu.with_memory_space_constraint(x, pltpu.HBM)


def fetched(pairs, sems):
    copies = []
    for at, (source, target) in enumerate(pairs):
        copy = pltpu.make_async_copy(source, target, sems.at[at])
        copy.start()
        copies.append(copy)
    return copies


def up_kernel(
    rhs_hbm,
    cols_hbm,
    leaf_hbm,
    inner_hbm,
    tree_hbm,
    rhs,
    tree,
    coeffs,
    second,
    first,
    block,
    packet,
    outward,
    cols,
    leaf_tr,
    inner_tr,
    sems,
):
    half = rhs.shape[1] // 2
    size = rhs.shape[1] // 8
    wide = 2 * size
    pairs = []
    for side in range(2):
        span = pl.ds(side * half, half)
        pairs += [(rhs_hbm.at[:, span], rhs.at[:, span]), (cols_hbm.at[:, span], cols.at[:, span])]
    pairs += [(leaf_hbm, leaf_tr), (inner_hbm, inner_tr), (tree_hbm, tree)]
    copies = fetched(pairs, sems)
    parts = []
    for leaf in range(8):
        if leaf % 4 == 0:
            copies[leaf // 2].wait()
            copies[leaf // 2 + 1].wait()
        span = slice(leaf * size, (leaf + 1) * size)
        parts.append(
            lax.dot_general(rhs[:, span], cols[:, span], TURNED, preferred_element_type=F32)
        )
    copies[4].wait()
    copies[5].wait()
    ups = []
    for pair in range(4):
        both = jnp.concatenate(parts[2 * pair : 2 * pair + 2], axis=1)
        coeffs[:, pair * 128 : (pair + 1) * 128] = both
        ups.append(dot3(both, leaf_tr[pair]))
    left = jnp.concatenate(ups[:2], axis=1)
    right = jnp.concatenate(ups[2:], axis=1)
    second[:, :128] = left
    second[:, 128:] = right
    both = jnp.concatenate([dot3(left, inner_tr[1]), dot3(right, inner_tr[2])], axis=1)
    first[...] = both
    total = dot3(both, inner_tr[0])
    block[...] = total
    packet[:, :128] = jnp.concatenate(halves(total), axis=1)
    odd = lax.rem(lax.axis_index("leaf"), 2)
    inner_side = pl.multiple_of((1 - odd) * (rhs.shape[1] - wide), wide)
    outer_side = pl.multiple_of(odd * (rhs.shape[1] - wide), wide)
    packet[:, 128:] = rhs[:, pl.ds(inner_side, wide)]
    outward[...] = rhs[:, pl.ds(outer_side, wide)]
    copies[6].wait()


def run_up(rhs, cols, leaf_tr, inner_tr, tree_tr):
    rows, width = rhs.shape
    skel = cols.shape[0]
    wide = width // 4
    tables = (cols, leaf_tr, inner_tr)
    return pl.pallas_call(
        up_kernel,
        in_specs=[ANY] * 5,
        out_specs=[VMEM] * 8,
        out_shape=[
            pltpu.VMEM(rhs.shape, rhs.dtype),
            pltpu.VMEM(tree_tr.shape, F32),
            pltpu.VMEM((rows, 8 * skel), F32),
            pltpu.VMEM((rows, 4 * skel), F32),
            pltpu.VMEM((rows, 2 * skel), F32),
            pltpu.VMEM((rows, skel), F32),
            pltpu.VMEM((rows, 2 * skel + wide), BF16),
            pltpu.VMEM((rows, wide), BF16),
        ],
        scratch_shapes=[pltpu.VMEM(x.shape, x.dtype) for x in tables]
        + [pltpu.SemaphoreType.DMA((7,))],
        compiler_params=limit(8),
        cost_estimate=LIGHT,
        name="up",
    )(*map(in_hbm, (rhs, cols, leaf_tr, inner_tr, tree_tr)))


def join_kernel(spans, *refs):
    refs, (out, sems) = refs[:-2], refs[-2:]
    pairs = []
    column = 0
    for part, (start, width) in zip(refs, spans):
        pairs.append((part.at[:, pl.ds(start, width)], out.at[:, pl.ds(column, width)]))
        column += width
    for copy in fetched(pairs, sems):
        copy.wait()


def run_join(parts, after=()):
    spans = [part[1:] for part in parts]
    arrays = [part[0] for part in parts]
    return pl.pallas_call(
        functools.partial(join_kernel, spans),
        in_specs=[ANY] * (len(parts) + len(after)),
        out_specs=VMEM,
        out_shape=pltpu.VMEM((arrays[0].shape[0], sum(w for _, w in spans)), arrays[0].dtype),
        scratch_shapes=[pltpu.SemaphoreType.DMA((len(parts),))],
        compiler_params=limit(1),
        cost_estimate=LIGHT,
        name="join",
    )(*arrays, *after)


def choose(table, wanted, picked):
    skel, _, nodes = table.shape
    select = (wanted == lax.broadcasted_iota(jnp.int32, (16, nodes), 1)).astype(BF16)
    dot = functools.partial(
        lax.dot_general, select, dimension_numbers=TURNED, preferred_element_type=F32
    )
    group = 4
    for k in range(0, skel, group):
        top, low = halves(table[k : k + group].reshape(group * skel, nodes))
        rows = dot(top) + dot(low)
        for at in range(group):
            picked[pl.ds(16 * (k + at), 16), :] = rows[:, at * skel : (at + 1) * skel]


def node_rows(nodes):
    return lax.broadcasted_iota(jnp.int32, (16, nodes), 0)


def pick_kernel(depth, tree, out, picked):
    skel, _, nodes = tree.shape
    heap = lax.axis_size("leaf") + lax.axis_index("leaf")
    row = node_rows(nodes)
    choose(tree, (lax.shift_right_logical(heap, row >> 1) ^ (row & 1)) - 2, picked)
    for bit in range(depth - 1):
        for side in range(2):
            out[bit, side * skel : (side + 1) * skel, :] = picked[
                pl.ds(2 * bit + side, skel, stride=16), :
            ]


def run_pick(depth, tree):
    skel = tree.shape[0]
    return pl.pallas_call(
        functools.partial(pick_kernel, depth),
        in_specs=[VMEM],
        out_specs=VMEM,
        out_shape=pltpu.VMEM((depth - 1, 2 * skel, skel), F32),
        scratch_shapes=[pltpu.VMEM((16 * skel, skel), F32)],
        compiler_params=limit(6),
        cost_estimate=LIGHT,
        name="pick",
    )(tree)


def first_lift_kernel(current, packet, mats, *rest):
    out, other = rest[-2:]
    skel = current.shape[1]
    sibling = packet[:, :skel].astype(F32) + packet[:, skel : 2 * skel].astype(F32)
    other[...] = sibling
    out[...] = dot3(jnp.concatenate([current[...], sibling], axis=1), mats[0])


def run_first_lift(current, packet, mats, after):
    return pl.pallas_call(
        first_lift_kernel,
        in_specs=[VMEM] * 3 + [ANY] * len(after),
        out_specs=[VMEM] * 2,
        out_shape=[pltpu.VMEM(current.shape, F32)] * 2,
        compiler_params=limit(1),
        cost_estimate=work(LIFT_WORK[0]),
        name="lift",
    )(current, packet, mats, *after)


def lift_kernel(bit, current, other, mats, *rest):
    out = rest[-1]
    skel = mats.shape[-1]
    both = jnp.concatenate([current[:, :skel], other[:, :skel]], axis=1)
    if out.shape[1] > skel:
        out[...] = jnp.zeros_like(out)
    out[:, :skel] = dot3(both, mats[bit])


def run_lift(bit, current, other, mats, after, width):
    return pl.pallas_call(
        functools.partial(lift_kernel, bit),
        in_specs=[VMEM] * 3 + [ANY] * len(after),
        out_specs=VMEM,
        out_shape=pltpu.VMEM((current.shape[0], width), F32),
        compiler_params=limit(1),
        cost_estimate=work(LIFT_WORK[bit]),
        name="lift",
    )(current, other, mats, *after)


def prep_kernel(
    coeffs,
    second,
    first,
    after,
    leaf_tr_hbm,
    leaf_cp_hbm,
    inner_tr_hbm,
    inner_cp_hbm,
    tree_hbm,
    local_ref,
    reach_ref,
    tree,
    leaf_tr,
    leaf_cp,
    inner_tr,
    inner_cp,
    sems,
):
    del after
    copies = fetched(
        [
            (inner_cp_hbm, inner_cp),
            (inner_tr_hbm, inner_tr),
            (leaf_cp_hbm, leaf_cp),
            (leaf_tr_hbm, leaf_tr),
            (tree_hbm, tree),
        ],
        sems,
    )

    def coupled(values, table):
        a = dot3(values[:, 64:], table[:64], TURNED)
        b = dot3(values[:, :64], table[64:], TURNED)
        return jnp.concatenate([a, b], axis=1)

    for copy in copies[:4]:
        copy.wait()
    tops = coupled(first[...], inner_cp[0])
    mids = []
    for side in range(2):
        own = coupled(second[:, side * 128 : (side + 1) * 128], inner_cp[1 + side])
        mids.append(own + dot3(tops[:, side * 64 : (side + 1) * 64], inner_tr[1 + side], TURNED))
    reach_top = inner_tr[0]
    for pair in range(4):
        side = pair // 2
        low = (pair % 2) * 64
        own = coupled(coeffs[:, pair * 128 : (pair + 1) * 128], leaf_cp[pair])
        own = own + dot3(mids[side][:, low : low + 64], leaf_tr[pair], TURNED)
        local_ref[:, pair * 128 : (pair + 1) * 128] = own
        if pair % 2 == 0:
            reach_mid = dot3(inner_tr[1 + side], reach_top[side * 64 : (side + 1) * 64])
        reach_ref[pair * 128 : (pair + 1) * 128, :] = dot3(leaf_tr[pair], reach_mid[low : low + 64])
    copies[4].wait()


def run_prep(coeffs, second, first, leaf_tr, leaf_cp, inner_tr, inner_cp, tree_cp, after):
    rows = coeffs.shape[0]
    skel = first.shape[1] // 2
    tables = (leaf_tr, leaf_cp, inner_tr, inner_cp)
    return pl.pallas_call(
        prep_kernel,
        in_specs=[VMEM] * 3 + [ANY] * 6,
        out_specs=[VMEM] * 3,
        out_shape=[
            pltpu.VMEM((rows, 8 * skel), F32),
            pltpu.VMEM((8 * skel, skel), F32),
            pltpu.VMEM(tree_cp.shape, F32),
        ],
        scratch_shapes=[pltpu.VMEM(x.shape, F32) for x in tables] + [pltpu.SemaphoreType.DMA((5,))],
        compiler_params=limit(6),
        cost_estimate=LIGHT,
        name="prep",
    )(coeffs, second, first, after, *map(in_hbm, (*tables, tree_cp)))


def turn_kernel(depth, mats, tree, after, out, picked):
    del after
    skel, _, nodes = tree.shape
    heap = lax.axis_size("leaf") + lax.axis_index("leaf")
    choose(tree, lax.shift_right_logical(heap, node_rows(nodes)) - 2, picked)
    chain = None
    for bit in range(depth):
        couple = picked[pl.ds(bit, skel, stride=16), :]
        out[bit] = couple if chain is None else dot3(chain, couple)
        if bit + 1 < depth:
            step = mats[bit, :skel]
            chain = step if chain is None else dot3(chain, step)


def run_turn(depth, mats, tree, after):
    skel = tree.shape[0]
    return pl.pallas_call(
        functools.partial(turn_kernel, depth),
        in_specs=[VMEM] * 2 + [ANY],
        out_specs=VMEM,
        out_shape=pltpu.VMEM((depth, skel, skel), F32),
        scratch_shapes=[pltpu.VMEM((16 * skel, skel), F32)],
        compiler_params=limit(6),
        cost_estimate=LIGHT,
        name="turn",
    )(mats, tree, after)


def near_kernel(index, own, mate, far, edge, edge_far, relay, diag, near, after, *rest):
    del after
    outs, grid = rest[:4], rest[4]
    rows, width = own.shape
    count, part, size = diag.shape
    wide = 2 * size
    odd = lax.rem(lax.axis_index("leaf"), 2)
    inner = pl.multiple_of((1 - odd) * (width + wide), wide)
    outer = pl.multiple_of(odd * (width + wide), wide)

    def place(source, start, length, group, column):
        target = (pl.ds(group * rows, rows), pl.ds(column, length))
        grid[target] = source[:, start : start + length]

    place(own, 0, width, 0, wide)
    place(mate, 0, width, 1, wide)
    place(far, 0, width, 2, wide)
    place(relay, 0, width, 3, wide)
    for group, (source, start) in enumerate(
        ((edge, 0), (relay, width), (edge_far, 0), (relay, width + 2 * wide))
    ):
        place(source, start, wide, group, inner)
        place(source, start + wide, wide, group, outer)
    base = lax.axis_index("leaf") * count - 2
    dot = functools.partial(
        lax.dot_general, dimension_numbers=TURNED, preferred_element_type=F32
    )
    for leaf in range(count):
        total = dot(grid[:, (leaf + 2) * size : (leaf + 3) * size], diag[leaf])
        for j in range(near.shape[1]):
            column = pl.multiple_of((index[j, leaf] - base) * size, size)
            total = total + dot(grid[:, pl.ds(column, size)], near[leaf, j])
        for group, out in enumerate(outs):
            block = total[group * rows : (group + 1) * rows]
            out[:, leaf * part : (leaf + 1) * part] = block.astype(out.dtype)


def run_near(index, own, mate, far, edge, edge_far, relay, diag, near, after):
    rows, width = own.shape
    count, part, size = diag.shape
    return pl.pallas_call(
        near_kernel,
        in_specs=[pl.BlockSpec(memory_space=pltpu.SMEM)] + [VMEM] * 8 + [ANY],
        out_specs=[VMEM] * 4,
        out_shape=[pltpu.VMEM((rows, count * part), F32)]
        + [pltpu.VMEM((rows, count * part), BF16)] * 3,
        scratch_shapes=[pltpu.VMEM((4 * rows, width + 4 * size), BF16)],
        compiler_params=limit(12),
        cost_estimate=LIGHT,
        name="near",
    )(index, own, mate, far, edge, edge_far, relay, diag, near, after)


def settle_kernel(*refs):
    others, (turn, reach, local, leaf, final) = refs[:-5], refs[-5:]
    skel = turn.shape[1]
    total = None
    for bit, other in enumerate(others):
        term = dot3(other[:, :skel], turn[bit], TURNED)
        total = term if total is None else total + term
    leaf[...] = local[...] + dot3(total, reach[...], TURNED)
    final[...] = dot3(reach[...], turn[len(others)])


def run_settle(others, turn, reach, local):
    return pl.pallas_call(
        settle_kernel,
        in_specs=[VMEM] * (len(others) + 3),
        out_specs=[VMEM] * 2,
        out_shape=[pltpu.VMEM(local.shape, F32), pltpu.VMEM(reach.shape, F32)],
        compiler_params=limit(2),
        cost_estimate=LIGHT,
        name="settle",
    )(*others, turn, reach, local)


def last_kernel(groups, other, final, local, basis, *rest):
    close, (out_hbm, out, sems) = rest[:-3], rest[-3:]
    skel = other.shape[1]
    count = local.shape[1] // skel
    size = basis.shape[1] // count
    part = close[0].shape[1] // count
    leaf = (local[...] + dot3(other[...], final[...], TURNED)).astype(BF16)
    place = lax.axis_index("rhs")
    copies = []
    for at in range(count):
        span = slice(at * size, (at + 1) * size)
        out[:, span] = lax.dot_general(
            leaf[:, at * skel : (at + 1) * skel], basis[:, span], PLAIN, preferred_element_type=F32
        )
        for group, block in zip(groups, close):
            column = pl.multiple_of(at * size + (place ^ group) * part, part)
            here = pl.ds(column, part)
            out[:, here] = out[:, here] + block[:, at * part : (at + 1) * part].astype(F32)
        if at % 2:
            here = pl.ds((at - 1) * size, 2 * size)
            copy = pltpu.make_async_copy(out.at[:, here], out_hbm.at[:, here], sems.at[at // 2])
            copy.start()
            copies.append(copy)
    for copy in copies:
        copy.wait()


def run_last(other, final, local, basis, close):
    rows = local.shape[0]
    groups = list(close)
    return pl.pallas_call(
        functools.partial(last_kernel, groups),
        in_specs=[VMEM] * (len(close) + 4),
        out_specs=ANY,
        out_shape=jax.ShapeDtypeStruct((rows, basis.shape[1]), F32),
        scratch_shapes=[
            pltpu.VMEM((rows, basis.shape[1]), F32),
            pltpu.SemaphoreType.DMA((local.shape[1] // other.shape[1] // 2,)),
        ],
        compiler_params=limit(6),
        cost_estimate=LIGHT,
        name="last",
    )(other, final, local, basis, *close.values())


def local(
    rhs_block,
    col_basis,
    row_basis,
    leaf_transfer,
    leaf_coupling,
    inner_transfer,
    inner_coupling,
    tree_transfer,
    tree_coupling,
    diag_blocks,
    near_blocks,
    near_leaves,
):
    width = rhs_block.shape[1]
    count = leaf_transfer.shape[0]
    wide = 2 * (width // count)
    skel = col_basis.shape[0]
    span = lax.axis_size("leaf")
    ranks = lax.axis_size("rhs")
    depth = span.bit_length() - 1
    leaf_tr = leaf_transfer.reshape(count // 2, 2 * skel, skel)
    leaf_cp = leaf_coupling.reshape(count // 2, 2 * skel, skel)
    inner_tr = inner_transfer.reshape(count // 2 - 1, 2 * skel, skel)
    inner_cp = inner_coupling.reshape(count // 2 - 1, 2 * skel, skel)

    far = swapped(rhs_block, "rhs", 2)
    mate = swapped(rhs_block, "rhs", 1)
    own, tree, coeffs, second, first, block, packet, outward = run_up(
        rhs_block, col_basis, leaf_tr, inner_tr, jnp.transpose(tree_transfer, (1, 2, 0))
    )

    packet = swapped(packet, "leaf", 1)
    mats = run_pick(depth, tree)
    pairs = [(i, i + 1) for i in range(1, span - 1, 2)]
    outward = lax.ppermute(outward, "leaf", pairs + [(j, i) for i, j in pairs])
    current, other = run_first_lift(block, packet, mats, [])
    others = [other]

    def step(current, beside, width=skel):
        bit = len(others)
        others.append(swapped(current, "leaf", 1 << bit))
        return run_lift(bit, current, others[-1], mats, beside, width)

    local_part, reach, tree = run_prep(
        coeffs,
        second,
        first,
        leaf_tr,
        leaf_cp,
        inner_tr,
        inner_cp,
        jnp.transpose(tree_coupling, (1, 2, 0)),
        current,
    )
    current = step(current, [reach])
    edge = run_join([(packet, 2 * skel, wide), (outward, 0, wide)], [current])
    edge_far = swapped(edge, "rhs", 2)
    current = step(current, [edge])
    turn = run_turn(depth, mats, tree, current)
    joined = run_join(
        [(far, 0, width), (edge, 0, 2 * wide), (edge_far, 0, 2 * wide)], [current]
    )
    relay = swapped(joined, "rhs", 1)
    current = step(current, [joined, turn])
    close = run_near(
        near_leaves.T, own, mate, far, edge, edge_far, relay, diag_blocks, near_blocks, current
    )
    current = step(current, close[:1])
    close = {k: swapped(close[k], "rhs", k) if k else close[0] for k in (0, 2, 3, 1)}
    leaf_part, final = run_settle(others, turn, reach, local_part)
    other = swapped(current, "leaf", 1 << len(others))
    return run_last(other, final, leaf_part, row_basis, close)


def solution(mesh):
    in_specs = (
        P("rhs", "leaf"),
        P(None, "leaf"),
        P(None, "leaf"),
        P("leaf", None, None),
        P("leaf", None, None),
        P("leaf", None, None, None),
        P("leaf", None, None, None),
        P(),
        P(),
        P("leaf", "rhs", None),
        P("leaf", None, "rhs", None),
        P("leaf", None),
    )
    out_specs = P("rhs", "leaf")
    return jax.shard_map(local, mesh=mesh, in_specs=in_specs, out_specs=out_specs, check_vma=False)
```

```python
import functools

import jax
import jax.numpy as jnp
from jax import lax
from jax.experimental import pallas as pl
from jax.experimental.pallas import tpu as pltpu
from jax.sharding import PartitionSpec as P

F32 = jnp.float32
BF16 = jnp.bfloat16
VMEM = pl.BlockSpec(memory_space=pltpu.VMEM)
ANY = pl.BlockSpec(memory_space=pl.ANY)
PLAIN = (((1,), (0,)), ((), ()))
TURNED = (((1,), (1,)), ((), ()))


def work(flops):
    return pl.CostEstimate(flops=flops, bytes_accessed=0, transcendentals=0)


LIFT_WORK = (20_000_000_000, 500_000_000, 2_500_000_000, 20_000_000_000, 20_000_000_000)
LIGHT = work(0)


def halves(x):
    top = x.astype(BF16)
    return top, (x - top.astype(F32)).astype(BF16)


def dot3(a, b, dims=PLAIN):
    ah, al = halves(a)
    bh, bl = halves(b)
    dot = functools.partial(lax.dot_general, dimension_numbers=dims, preferred_element_type=F32)
    return dot(ah, bh) + (dot(ah, bl) + dot(al, bh))


def swapped(x, axis, bit):
    count = lax.axis_size(axis)
    return lax.ppermute(x, axis, [(i, i ^ bit) for i in range(count)])


def limit(mib):
    return pltpu.CompilerParams(vmem_limit_bytes=mib << 20)


def in_hbm(x):
    return pltpu.with_memory_space_constraint(x, pltpu.HBM)


def fetched(pairs, sems):
    copies = []
    for at, (source, target) in enumerate(pairs):
        copy = pltpu.make_async_copy(source, target, sems.at[at])
        copy.start()
        copies.append(copy)
    return copies


def up_kernel(
    rhs_hbm,
    cols_hbm,
    leaf_hbm,
    inner_hbm,
    tree_hbm,
    rhs,
    tree,
    coeffs,
    second,
    first,
    block,
    packet,
    outward,
    cols,
    leaf_tr,
    inner_tr,
    sems,
):
    size = rhs.shape[1] // 8
    wide = 2 * size
    pairs = [(rhs_hbm, rhs), (cols_hbm, cols), (leaf_hbm, leaf_tr), (inner_hbm, inner_tr), (tree_hbm, tree)]
    copies = fetched(pairs, sems)
    parts = []
    for leaf in range(8):
        if leaf == 0:
            copies[0].wait()
            copies[1].wait()
        span = slice(leaf * size, (leaf + 1) * size)
        parts.append(
            lax.dot_general(rhs[:, span], cols[:, span], TURNED, preferred_element_type=F32)
        )
    copies[2].wait()
    copies[3].wait()
    ups = []
    for pair in range(4):
        both = jnp.concatenate(parts[2 * pair : 2 * pair + 2], axis=1)
        coeffs[:, pair * 128 : (pair + 1) * 128] = both
        ups.append(dot3(both, leaf_tr[pair]))
    left = jnp.concatenate(ups[:2], axis=1)
    right = jnp.concatenate(ups[2:], axis=1)
    second[:, :128] = left
    second[:, 128:] = right
    both = jnp.concatenate([dot3(left, inner_tr[1]), dot3(right, inner_tr[2])], axis=1)
    first[...] = both
    total = dot3(both, inner_tr[0])
    block[...] = total
    packet[:, :128] = jnp.concatenate(halves(total), axis=1)
    odd = lax.rem(lax.axis_index("leaf"), 2)
    inner_side = pl.multiple_of((1 - odd) * (rhs.shape[1] - wide), wide)
    outer_side = pl.multiple_of(odd * (rhs.shape[1] - wide), wide)
    packet[:, 128:] = rhs[:, pl.ds(inner_side, wide)]
    outward[...] = rhs[:, pl.ds(outer_side, wide)]
    copies[4].wait()


def run_up(rhs, cols, leaf_tr, inner_tr, tree_tr):
    rows, width = rhs.shape
    skel = cols.shape[0]
    wide = width // 4
    tables = (cols, leaf_tr, inner_tr)
    return pl.pallas_call(
        up_kernel,
        in_specs=[ANY] * 5,
        out_specs=[VMEM] * 8,
        out_shape=[
            pltpu.VMEM(rhs.shape, rhs.dtype),
            pltpu.VMEM(tree_tr.shape, F32),
            pltpu.VMEM((rows, 8 * skel), F32),
            pltpu.VMEM((rows, 4 * skel), F32),
            pltpu.VMEM((rows, 2 * skel), F32),
            pltpu.VMEM((rows, skel), F32),
            pltpu.VMEM((rows, 2 * skel + wide), BF16),
            pltpu.VMEM((rows, wide), BF16),
        ],
        scratch_shapes=[pltpu.VMEM(x.shape, x.dtype) for x in tables]
        + [pltpu.SemaphoreType.DMA((5,))],
        compiler_params=limit(8),
        cost_estimate=LIGHT,
        name="up",
    )(*map(in_hbm, (rhs, cols, leaf_tr, inner_tr, tree_tr)))


def join_kernel(spans, *refs):
    refs, (out, sems) = refs[:-2], refs[-2:]
    pairs = []
    column = 0
    for part, (start, width) in zip(refs, spans):
        pairs.append((part.at[:, pl.ds(start, width)], out.at[:, pl.ds(column, width)]))
        column += width
    for copy in fetched(pairs, sems):
        copy.wait()


def run_join(parts, after=()):
    spans = [part[1:] for part in parts]
    arrays = [part[0] for part in parts]
    return pl.pallas_call(
        functools.partial(join_kernel, spans),
        in_specs=[ANY] * (len(parts) + len(after)),
        out_specs=VMEM,
        out_shape=pltpu.VMEM((arrays[0].shape[0], sum(w for _, w in spans)), arrays[0].dtype),
        scratch_shapes=[pltpu.SemaphoreType.DMA((len(parts),))],
        compiler_params=limit(1),
        cost_estimate=LIGHT,
        name="join",
    )(*arrays, *after)


def choose(table, wanted, picked):
    skel, _, nodes = table.shape
    select = (wanted == lax.broadcasted_iota(jnp.int32, (16, nodes), 1)).astype(BF16)
    dot = functools.partial(
        lax.dot_general, select, dimension_numbers=TURNED, preferred_element_type=F32
    )
    group = 4
    for k in range(0, skel, group):
        top, low = halves(table[k : k + group].reshape(group * skel, nodes))
        rows = dot(top) + dot(low)
        for at in range(group):
            picked[pl.ds(16 * (k + at), 16), :] = rows[:, at * skel : (at + 1) * skel]


def node_rows(nodes):
    return lax.broadcasted_iota(jnp.int32, (16, nodes), 0)


def pick_kernel(depth, tree, out, picked):
    skel, _, nodes = tree.shape
    heap = lax.axis_size("leaf") + lax.axis_index("leaf")
    row = node_rows(nodes)
    choose(tree, (lax.shift_right_logical(heap, row >> 1) ^ (row & 1)) - 2, picked)
    for bit in range(depth - 1):
        for side in range(2):
            out[bit, side * skel : (side + 1) * skel, :] = picked[
                pl.ds(2 * bit + side, skel, stride=16), :
            ]


def run_pick(depth, tree):
    skel = tree.shape[0]
    return pl.pallas_call(
        functools.partial(pick_kernel, depth),
        in_specs=[VMEM],
        out_specs=VMEM,
        out_shape=pltpu.VMEM((depth - 1, 2 * skel, skel), F32),
        scratch_shapes=[pltpu.VMEM((16 * skel, skel), F32)],
        compiler_params=limit(6),
        cost_estimate=LIGHT,
        name="pick",
    )(tree)


def first_lift_kernel(current, packet, mats, *rest):
    out, other = rest[-2:]
    skel = current.shape[1]
    sibling = packet[:, :skel].astype(F32) + packet[:, skel : 2 * skel].astype(F32)
    other[...] = sibling
    out[...] = dot3(jnp.concatenate([current[...], sibling], axis=1), mats[0])


def run_first_lift(current, packet, mats, after):
    return pl.pallas_call(
        first_lift_kernel,
        in_specs=[VMEM] * 3 + [ANY] * len(after),
        out_specs=[VMEM] * 2,
        out_shape=[pltpu.VMEM(current.shape, F32)] * 2,
        compiler_params=limit(1),
        cost_estimate=work(LIFT_WORK[0]),
        name="lift",
    )(current, packet, mats, *after)


def lift_kernel(bit, current, other, mats, *rest):
    out = rest[-1]
    skel = mats.shape[-1]
    both = jnp.concatenate([current[:, :skel], other[:, :skel]], axis=1)
    if out.shape[1] > skel:
        out[...] = jnp.zeros_like(out)
    out[:, :skel] = dot3(both, mats[bit])


def run_lift(bit, current, other, mats, after, width):
    return pl.pallas_call(
        functools.partial(lift_kernel, bit),
        in_specs=[VMEM] * 3 + [ANY] * len(after),
        out_specs=VMEM,
        out_shape=pltpu.VMEM((current.shape[0], width), F32),
        compiler_params=limit(1),
        cost_estimate=work(LIFT_WORK[bit]),
        name="lift",
    )(current, other, mats, *after)


def prep_kernel(
    coeffs,
    second,
    first,
    after,
    leaf_tr_hbm,
    leaf_cp_hbm,
    inner_tr_hbm,
    inner_cp_hbm,
    local_ref,
    reach_ref,
    leaf_tr,
    leaf_cp,
    inner_tr,
    inner_cp,
    sems,
):
    del after
    copies = fetched(
        [
            (inner_cp_hbm, inner_cp),
            (inner_tr_hbm, inner_tr),
            (leaf_cp_hbm, leaf_cp),
            (leaf_tr_hbm, leaf_tr),
        ],
        sems,
    )

    def coupled(values, table):
        a = dot3(values[:, 64:], table[:64], TURNED)
        b = dot3(values[:, :64], table[64:], TURNED)
        return jnp.concatenate([a, b], axis=1)

    for copy in copies:
        copy.wait()
    tops = coupled(first[...], inner_cp[0])
    mids = []
    for side in range(2):
        own = coupled(second[:, side * 128 : (side + 1) * 128], inner_cp[1 + side])
        mids.append(own + dot3(tops[:, side * 64 : (side + 1) * 64], inner_tr[1 + side], TURNED))
    reach_top = inner_tr[0]
    for pair in range(4):
        side = pair // 2
        low = (pair % 2) * 64
        own = coupled(coeffs[:, pair * 128 : (pair + 1) * 128], leaf_cp[pair])
        own = own + dot3(mids[side][:, low : low + 64], leaf_tr[pair], TURNED)
        local_ref[:, pair * 128 : (pair + 1) * 128] = own
        if pair % 2 == 0:
            reach_mid = dot3(inner_tr[1 + side], reach_top[side * 64 : (side + 1) * 64])
        reach_ref[pair * 128 : (pair + 1) * 128, :] = dot3(leaf_tr[pair], reach_mid[low : low + 64])


def run_prep(coeffs, second, first, leaf_tr, leaf_cp, inner_tr, inner_cp, after):
    rows = coeffs.shape[0]
    skel = first.shape[1] // 2
    tables = (leaf_tr, leaf_cp, inner_tr, inner_cp)
    return pl.pallas_call(
        prep_kernel,
        in_specs=[VMEM] * 3 + [ANY] * 5,
        out_specs=[VMEM] * 2,
        out_shape=[
            pltpu.VMEM((rows, 8 * skel), F32),
            pltpu.VMEM((8 * skel, skel), F32),
        ],
        scratch_shapes=[pltpu.VMEM(x.shape, F32) for x in tables] + [pltpu.SemaphoreType.DMA((4,))],
        compiler_params=limit(6),
        cost_estimate=LIGHT,
        name="prep",
    )(coeffs, second, first, after, *map(in_hbm, tables))


def turn_kernel(depth, mats, tree, after, out, picked):
    del after
    skel, _, nodes = tree.shape
    heap = lax.axis_size("leaf") + lax.axis_index("leaf")
    choose(tree, lax.shift_right_logical(heap, node_rows(nodes)) - 2, picked)
    chain = None
    for bit in range(depth):
        couple = picked[pl.ds(bit, skel, stride=16), :]
        out[bit] = couple if chain is None else dot3(chain, couple)
        if bit + 1 < depth:
            step = mats[bit, :skel]
            chain = step if chain is None else dot3(chain, step)


def run_turn(depth, mats, tree, after):
    skel = tree.shape[0]
    return pl.pallas_call(
        functools.partial(turn_kernel, depth),
        in_specs=[VMEM] * 2 + [ANY],
        out_specs=VMEM,
        out_shape=pltpu.VMEM((depth, skel, skel), F32),
        scratch_shapes=[pltpu.VMEM((16 * skel, skel), F32)],
        compiler_params=limit(6),
        cost_estimate=LIGHT,
        name="turn",
    )(mats, tree, after)


def near_kernel(index, own, mate, far, edge, edge_far, relay, diag, near, after, *rest):
    del after
    outs, grid = rest[:4], rest[4]
    rows, width = own.shape
    count, part, size = diag.shape
    wide = 2 * size
    odd = lax.rem(lax.axis_index("leaf"), 2)
    inner = pl.multiple_of((1 - odd) * (width + wide), wide)
    outer = pl.multiple_of(odd * (width + wide), wide)

    def place(source, start, length, group, column):
        target = (pl.ds(group * rows, rows), pl.ds(column, length))
        grid[target] = source[:, start : start + length]

    place(own, 0, width, 0, wide)
    place(mate, 0, width, 1, wide)
    place(far, 0, width, 2, wide)
    place(relay, 0, width, 3, wide)
    for group, (source, start) in enumerate(
        ((edge, 0), (relay, width), (edge_far, 0), (relay, width + 2 * wide))
    ):
        place(source, start, wide, group, inner)
        place(source, start + wide, wide, group, outer)
    base = lax.axis_index("leaf") * count - 2
    dot = functools.partial(
        lax.dot_general, dimension_numbers=TURNED, preferred_element_type=F32
    )
    for leaf in range(count):
        total = dot(grid[:, (leaf + 2) * size : (leaf + 3) * size], diag[leaf])
        for j in range(near.shape[1]):
            column = pl.multiple_of((index[j, leaf] - base) * size, size)
            total = total + dot(grid[:, pl.ds(column, size)], near[leaf, j])
        for group, out in enumerate(outs):
            block = total[group * rows : (group + 1) * rows]
            out[:, leaf * part : (leaf + 1) * part] = block.astype(out.dtype)


def run_near(index, own, mate, far, edge, edge_far, relay, diag, near, after):
    rows, width = own.shape
    count, part, size = diag.shape
    return pl.pallas_call(
        near_kernel,
        in_specs=[pl.BlockSpec(memory_space=pltpu.SMEM)] + [VMEM] * 8 + [ANY],
        out_specs=[VMEM] * 4,
        out_shape=[pltpu.VMEM((rows, count * part), F32)]
        + [pltpu.VMEM((rows, count * part), BF16)] * 3,
        scratch_shapes=[pltpu.VMEM((4 * rows, width + 4 * size), BF16)],
        compiler_params=limit(12),
        cost_estimate=LIGHT,
        name="near",
    )(index, own, mate, far, edge, edge_far, relay, diag, near, after)


def settle_kernel(*refs):
    others, (turn, reach, local, leaf, final) = refs[:-5], refs[-5:]
    skel = turn.shape[1]
    total = None
    for bit, other in enumerate(others):
        term = dot3(other[:, :skel], turn[bit], TURNED)
        total = term if total is None else total + term
    leaf[...] = local[...] + dot3(total, reach[...], TURNED)
    final[...] = dot3(reach[...], turn[len(others)])


def run_settle(others, turn, reach, local):
    return pl.pallas_call(
        settle_kernel,
        in_specs=[VMEM] * (len(others) + 3),
        out_specs=[VMEM] * 2,
        out_shape=[pltpu.VMEM(local.shape, F32), pltpu.VMEM(reach.shape, F32)],
        compiler_params=limit(2),
        cost_estimate=LIGHT,
        name="settle",
    )(*others, turn, reach, local)


def last_kernel(groups, other, final, local, basis, *rest):
    close, (out_hbm, out, sems) = rest[:-3], rest[-3:]
    skel = other.shape[1]
    count = local.shape[1] // skel
    size = basis.shape[1] // count
    part = close[0].shape[1] // count
    leaf = (local[...] + dot3(other[...], final[...], TURNED)).astype(BF16)
    place = lax.axis_index("rhs")
    copies = []
    for at in range(count):
        span = slice(at * size, (at + 1) * size)
        out[:, span] = lax.dot_general(
            leaf[:, at * skel : (at + 1) * skel], basis[:, span], PLAIN, preferred_element_type=F32
        )
        for group, block in zip(groups, close):
            column = pl.multiple_of(at * size + (place ^ group) * part, part)
            here = pl.ds(column, part)
            out[:, here] = out[:, here] + block[:, at * part : (at + 1) * part].astype(F32)
        if at % 2:
            here = pl.ds((at - 1) * size, 2 * size)
            copy = pltpu.make_async_copy(out.at[:, here], out_hbm.at[:, here], sems.at[at // 2])
            copy.start()
            copies.append(copy)
    for copy in copies:
        copy.wait()


def run_last(other, final, local, basis, close):
    rows = local.shape[0]
    groups = list(close)
    return pl.pallas_call(
        functools.partial(last_kernel, groups),
        in_specs=[VMEM] * (len(close) + 4),
        out_specs=ANY,
        out_shape=jax.ShapeDtypeStruct((rows, basis.shape[1]), F32),
        scratch_shapes=[
            pltpu.VMEM((rows, basis.shape[1]), F32),
            pltpu.SemaphoreType.DMA((local.shape[1] // other.shape[1] // 2,)),
        ],
        compiler_params=limit(6),
        cost_estimate=LIGHT,
        name="last",
    )(other, final, local, basis, *close.values())


def local(
    rhs_block,
    col_basis,
    row_basis,
    leaf_transfer,
    leaf_coupling,
    inner_transfer,
    inner_coupling,
    tree_transfer,
    tree_coupling,
    diag_blocks,
    near_blocks,
    near_leaves,
):
    width = rhs_block.shape[1]
    count = leaf_transfer.shape[0]
    wide = 2 * (width // count)
    skel = col_basis.shape[0]
    span = lax.axis_size("leaf")
    ranks = lax.axis_size("rhs")
    depth = span.bit_length() - 1
    leaf_tr = leaf_transfer.reshape(count // 2, 2 * skel, skel)
    leaf_cp = leaf_coupling.reshape(count // 2, 2 * skel, skel)
    inner_tr = inner_transfer.reshape(count // 2 - 1, 2 * skel, skel)
    inner_cp = inner_coupling.reshape(count // 2 - 1, 2 * skel, skel)

    far = swapped(rhs_block, "rhs", 2)
    mate = swapped(rhs_block, "rhs", 1)
    own, tree, coeffs, second, first, block, packet, outward = run_up(
        rhs_block, col_basis, leaf_tr, inner_tr, jnp.transpose(tree_transfer, (1, 2, 0))
    )

    packet = swapped(packet, "leaf", 1)
    mats = run_pick(depth, tree)
    pairs = [(i, i + 1) for i in range(1, span - 1, 2)]
    outward = lax.ppermute(outward, "leaf", pairs + [(j, i) for i, j in pairs])
    current, other = run_first_lift(block, packet, mats, [])
    others = [other]

    def step(current, beside, width=skel):
        bit = len(others)
        others.append(swapped(current, "leaf", 1 << bit))
        return run_lift(bit, current, others[-1], mats, beside, width)

    local_part, reach = run_prep(
        coeffs,
        second,
        first,
        leaf_tr,
        leaf_cp,
        inner_tr,
        inner_cp,
        current,
    )
    current = step(current, [reach])
    edge = run_join([(packet, 2 * skel, wide), (outward, 0, wide)], [current])
    edge_far = swapped(edge, "rhs", 2)
    current = step(current, [edge])
    turn = run_turn(depth, mats, jnp.transpose(tree_coupling, (1, 2, 0)), current)
    joined = run_join(
        [(far, 0, width), (edge, 0, 2 * wide), (edge_far, 0, 2 * wide)], [current]
    )
    relay = swapped(joined, "rhs", 1)
    current = step(current, [joined, turn])
    close = run_near(
        near_leaves.T, own, mate, far, edge, edge_far, relay, diag_blocks, near_blocks, current
    )
    current = step(current, close[:1])
    close = {k: swapped(close[k], "rhs", k) if k else close[0] for k in (0, 3, 2, 1)}
    leaf_part, final = run_settle(others, turn, reach, local_part)
    other = swapped(current, "leaf", 1 << len(others))
    return run_last(other, final, leaf_part, row_basis, close)


def solution(mesh):
    in_specs = (
        P("rhs", "leaf"),
        P(None, "leaf"),
        P(None, "leaf"),
        P("leaf", None, None),
        P("leaf", None, None),
        P("leaf", None, None, None),
        P("leaf", None, None, None),
        P(),
        P(),
        P("leaf", "rhs", None),
        P("leaf", None, "rhs", None),
        P("leaf", None),
    )
    out_specs = P("rhs", "leaf")
    return jax.shard_map(local, mesh=mesh, in_specs=in_specs, out_specs=out_specs, check_vma=False)
```

```python
import functools

import jax
import jax.numpy as jnp
from jax import lax
from jax.experimental import pallas as pl
from jax.experimental.pallas import tpu as pltpu
from jax.sharding import PartitionSpec as P

F32 = jnp.float32
BF16 = jnp.bfloat16
VMEM = pl.BlockSpec(memory_space=pltpu.VMEM)
ANY = pl.BlockSpec(memory_space=pl.ANY)
PLAIN = (((1,), (0,)), ((), ()))
TURNED = (((1,), (1,)), ((), ()))


def work(flops):
    return pl.CostEstimate(flops=flops, bytes_accessed=0, transcendentals=0)


LIFT_WORK = (20_000_000_000, 500_000_000, 2_500_000_000, 20_000_000_000, 20_000_000_000)
LIGHT = work(0)


def halves(x):
    top = x.astype(BF16)
    return top, (x - top.astype(F32)).astype(BF16)


def dot3(a, b, dims=PLAIN):
    ah, al = halves(a)
    bh, bl = halves(b)
    dot = functools.partial(lax.dot_general, dimension_numbers=dims, preferred_element_type=F32)
    return dot(ah, bh) + (dot(ah, bl) + dot(al, bh))


def swapped(x, axis, bit):
    count = lax.axis_size(axis)
    return lax.ppermute(x, axis, [(i, i ^ bit) for i in range(count)])


def limit(mib):
    return pltpu.CompilerParams(vmem_limit_bytes=mib << 20)


def in_hbm(x):
    return pltpu.with_memory_space_constraint(x, pltpu.HBM)


def fetched(pairs, sems):
    copies = []
    for at, (source, target) in enumerate(pairs):
        copy = pltpu.make_async_copy(source, target, sems.at[at])
        copy.start()
        copies.append(copy)
    return copies


def up_kernel(
    rhs_hbm,
    cols_hbm,
    leaf_hbm,
    inner_hbm,
    tree_hbm,
    rhs,
    tree,
    coeffs,
    second,
    first,
    block,
    packet,
    outward,
    cols,
    leaf_tr,
    inner_tr,
    sems,
):
    size = rhs.shape[1] // 8
    wide = 2 * size
    pairs = [(rhs_hbm, rhs), (cols_hbm, cols), (leaf_hbm, leaf_tr), (inner_hbm, inner_tr), (tree_hbm, tree)]
    copies = fetched(pairs, sems)
    parts = []
    for leaf in range(8):
        if leaf == 0:
            copies[0].wait()
            copies[1].wait()
        span = slice(leaf * size, (leaf + 1) * size)
        parts.append(
            lax.dot_general(rhs[:, span], cols[:, span], TURNED, preferred_element_type=F32)
        )
    copies[2].wait()
    copies[3].wait()
    ups = []
    for pair in range(4):
        both = jnp.concatenate(parts[2 * pair : 2 * pair + 2], axis=1)
        coeffs[:, pair * 128 : (pair + 1) * 128] = both
        ups.append(dot3(both, leaf_tr[pair]))
    left = jnp.concatenate(ups[:2], axis=1)
    right = jnp.concatenate(ups[2:], axis=1)
    second[:, :128] = left
    second[:, 128:] = right
    both = jnp.concatenate([dot3(left, inner_tr[1]), dot3(right, inner_tr[2])], axis=1)
    first[...] = both
    total = dot3(both, inner_tr[0])
    block[...] = total
    packet[:, :128] = jnp.concatenate(halves(total), axis=1)
    odd = lax.rem(lax.axis_index("leaf"), 2)
    inner_side = pl.multiple_of((1 - odd) * (rhs.shape[1] - wide), wide)
    outer_side = pl.multiple_of(odd * (rhs.shape[1] - wide), wide)
    packet[:, 128:] = rhs[:, pl.ds(inner_side, wide)]
    outward[...] = rhs[:, pl.ds(outer_side, wide)]
    copies[4].wait()


def run_up(rhs, cols, leaf_tr, inner_tr, tree_tr):
    rows, width = rhs.shape
    skel = cols.shape[0]
    wide = width // 4
    tables = (cols, leaf_tr, inner_tr)
    return pl.pallas_call(
        up_kernel,
        in_specs=[ANY] * 5,
        out_specs=[VMEM] * 8,
        out_shape=[
            pltpu.VMEM(rhs.shape, rhs.dtype),
            pltpu.VMEM(tree_tr.shape, F32),
            pltpu.VMEM((rows, 8 * skel), F32),
            pltpu.VMEM((rows, 4 * skel), F32),
            pltpu.VMEM((rows, 2 * skel), F32),
            pltpu.VMEM((rows, skel), F32),
            pltpu.VMEM((rows, 2 * skel + wide), BF16),
            pltpu.VMEM((rows, wide), BF16),
        ],
        scratch_shapes=[pltpu.VMEM(x.shape, x.dtype) for x in tables]
        + [pltpu.SemaphoreType.DMA((5,))],
        compiler_params=limit(8),
        cost_estimate=LIGHT,
        name="up",
    )(*map(in_hbm, (rhs, cols, leaf_tr, inner_tr, tree_tr)))


def join_kernel(spans, *refs):
    refs, (out, sems) = refs[:-2], refs[-2:]
    pairs = []
    column = 0
    for part, (start, width) in zip(refs, spans):
        pairs.append((part.at[:, pl.ds(start, width)], out.at[:, pl.ds(column, width)]))
        column += width
    for copy in fetched(pairs, sems):
        copy.wait()


def run_join(parts, after=()):
    spans = [part[1:] for part in parts]
    arrays = [part[0] for part in parts]
    return pl.pallas_call(
        functools.partial(join_kernel, spans),
        in_specs=[ANY] * (len(parts) + len(after)),
        out_specs=VMEM,
        out_shape=pltpu.VMEM((arrays[0].shape[0], sum(w for _, w in spans)), arrays[0].dtype),
        scratch_shapes=[pltpu.SemaphoreType.DMA((len(parts),))],
        compiler_params=limit(1),
        cost_estimate=LIGHT,
        name="join",
    )(*arrays, *after)


def choose(table, wanted, picked):
    skel, _, nodes = table.shape
    select = (wanted == lax.broadcasted_iota(jnp.int32, (16, nodes), 1)).astype(BF16)
    dot = functools.partial(
        lax.dot_general, select, dimension_numbers=TURNED, preferred_element_type=F32
    )
    group = 4
    for k in range(0, skel, group):
        top, low = halves(table[k : k + group].reshape(group * skel, nodes))
        rows = dot(top) + dot(low)
        for at in range(group):
            picked[pl.ds(16 * (k + at), 16), :] = rows[:, at * skel : (at + 1) * skel]


def node_rows(nodes):
    return lax.broadcasted_iota(jnp.int32, (16, nodes), 0)


def pick_kernel(depth, tree, out, picked):
    skel, _, nodes = tree.shape
    heap = lax.axis_size("leaf") + lax.axis_index("leaf")
    row = node_rows(nodes)
    choose(tree, (lax.shift_right_logical(heap, row >> 1) ^ (row & 1)) - 2, picked)
    for bit in range(depth - 1):
        for side in range(2):
            out[bit, side * skel : (side + 1) * skel, :] = picked[
                pl.ds(2 * bit + side, skel, stride=16), :
            ]


def run_pick(depth, tree):
    skel = tree.shape[0]
    return pl.pallas_call(
        functools.partial(pick_kernel, depth),
        in_specs=[VMEM],
        out_specs=VMEM,
        out_shape=pltpu.VMEM((depth - 1, 2 * skel, skel), F32),
        scratch_shapes=[pltpu.VMEM((16 * skel, skel), F32)],
        compiler_params=limit(6),
        cost_estimate=LIGHT,
        name="pick",
    )(tree)


def first_lift_kernel(current, packet, mats, *rest):
    out, other = rest[-2:]
    skel = current.shape[1]
    sibling = packet[:, :skel].astype(F32) + packet[:, skel : 2 * skel].astype(F32)
    other[...] = sibling
    out[...] = dot3(jnp.concatenate([current[...], sibling], axis=1), mats[0])


def run_first_lift(current, packet, mats, after):
    return pl.pallas_call(
        first_lift_kernel,
        in_specs=[VMEM] * 3 + [ANY] * len(after),
        out_specs=[VMEM] * 2,
        out_shape=[pltpu.VMEM(current.shape, F32)] * 2,
        compiler_params=limit(1),
        cost_estimate=work(LIFT_WORK[0]),
        name="lift",
    )(current, packet, mats, *after)


def lift_kernel(bit, current, other, mats, *rest):
    out = rest[-1]
    skel = mats.shape[-1]
    both = jnp.concatenate([current[:, :skel], other[:, :skel]], axis=1)
    if out.shape[1] > skel:
        out[...] = jnp.zeros_like(out)
    out[:, :skel] = dot3(both, mats[bit])


def run_lift(bit, current, other, mats, after, width):
    return pl.pallas_call(
        functools.partial(lift_kernel, bit),
        in_specs=[VMEM] * 3 + [ANY] * len(after),
        out_specs=VMEM,
        out_shape=pltpu.VMEM((current.shape[0], width), F32),
        compiler_params=limit(1),
        cost_estimate=work(LIFT_WORK[bit]),
        name="lift",
    )(current, other, mats, *after)


def prep_kernel(
    coeffs,
    second,
    first,
    after,
    leaf_tr_hbm,
    leaf_cp_hbm,
    inner_tr_hbm,
    inner_cp_hbm,
    local_ref,
    reach_ref,
    leaf_tr,
    leaf_cp,
    inner_tr,
    inner_cp,
    sems,
):
    del after
    copies = fetched(
        [
            (inner_cp_hbm, inner_cp),
            (inner_tr_hbm, inner_tr),
            (leaf_cp_hbm, leaf_cp),
            (leaf_tr_hbm, leaf_tr),
        ],
        sems,
    )

    def coupled(values, table):
        rows = values.shape[0]
        both = dot3(jnp.concatenate([values[:, 64:], values[:, :64]], axis=0), table, TURNED)
        return jnp.concatenate([both[:rows, :64], both[rows:, 64:]], axis=1)

    for copy in copies:
        copy.wait()
    tops = coupled(first[...], inner_cp[0])
    mids = []
    for side in range(2):
        own = coupled(second[:, side * 128 : (side + 1) * 128], inner_cp[1 + side])
        mids.append(own + dot3(tops[:, side * 64 : (side + 1) * 64], inner_tr[1 + side], TURNED))
    reach_top = inner_tr[0]
    for pair in range(4):
        side = pair // 2
        low = (pair % 2) * 64
        own = coupled(coeffs[:, pair * 128 : (pair + 1) * 128], leaf_cp[pair])
        own = own + dot3(mids[side][:, low : low + 64], leaf_tr[pair], TURNED)
        local_ref[:, pair * 128 : (pair + 1) * 128] = own
        if pair % 2 == 0:
            reach_mid = dot3(inner_tr[1 + side], reach_top[side * 64 : (side + 1) * 64])
        reach_ref[pair * 128 : (pair + 1) * 128, :] = dot3(leaf_tr[pair], reach_mid[low : low + 64])


def run_prep(coeffs, second, first, leaf_tr, leaf_cp, inner_tr, inner_cp, after):
    rows = coeffs.shape[0]
    skel = first.shape[1] // 2
    tables = (leaf_tr, leaf_cp, inner_tr, inner_cp)
    return pl.pallas_call(
        prep_kernel,
        in_specs=[VMEM] * 3 + [ANY] * 5,
        out_specs=[VMEM] * 2,
        out_shape=[
            pltpu.VMEM((rows, 8 * skel), F32),
            pltpu.VMEM((8 * skel, skel), F32),
        ],
        scratch_shapes=[pltpu.VMEM(x.shape, F32) for x in tables] + [pltpu.SemaphoreType.DMA((4,))],
        compiler_params=limit(6),
        cost_estimate=LIGHT,
        name="prep",
    )(coeffs, second, first, after, *map(in_hbm, tables))


def turn_kernel(depth, mats, tree, after, out, picked):
    del after
    skel, _, nodes = tree.shape
    heap = lax.axis_size("leaf") + lax.axis_index("leaf")
    choose(tree, lax.shift_right_logical(heap, node_rows(nodes)) - 2, picked)
    chain = None
    for bit in range(depth):
        couple = picked[pl.ds(bit, skel, stride=16), :]
        out[bit] = couple if chain is None else dot3(chain, couple)
        if bit + 1 < depth:
            step = mats[bit, :skel]
            chain = step if chain is None else dot3(chain, step)


def run_turn(depth, mats, tree, after):
    skel = tree.shape[0]
    return pl.pallas_call(
        functools.partial(turn_kernel, depth),
        in_specs=[VMEM] * 2 + [ANY],
        out_specs=VMEM,
        out_shape=pltpu.VMEM((depth, skel, skel), F32),
        scratch_shapes=[pltpu.VMEM((16 * skel, skel), F32)],
        compiler_params=limit(6),
        cost_estimate=LIGHT,
        name="turn",
    )(mats, tree, after)


def near_kernel(index, own, mate, far, edge, edge_far, relay, diag, near, after, *rest):
    del after
    outs, grid = rest[:4], rest[4]
    rows, width = own.shape
    count, part, size = diag.shape
    wide = 2 * size
    odd = lax.rem(lax.axis_index("leaf"), 2)
    inner = pl.multiple_of((1 - odd) * (width + wide), wide)
    outer = pl.multiple_of(odd * (width + wide), wide)

    def place(source, start, length, group, column):
        target = (pl.ds(group * rows, rows), pl.ds(column, length))
        grid[target] = source[:, start : start + length]

    place(own, 0, width, 0, wide)
    place(mate, 0, width, 1, wide)
    place(far, 0, width, 2, wide)
    place(relay, 0, width, 3, wide)
    for group, (source, start) in enumerate(
        ((edge, 0), (relay, width), (edge_far, 0), (relay, width + 2 * wide))
    ):
        place(source, start, wide, group, inner)
        place(source, start + wide, wide, group, outer)
    base = lax.axis_index("leaf") * count - 2
    dot = functools.partial(
        lax.dot_general, dimension_numbers=TURNED, preferred_element_type=F32
    )
    for leaf in range(count):
        total = dot(grid[:, (leaf + 2) * size : (leaf + 3) * size], diag[leaf])
        for j in range(near.shape[1]):
            column = pl.multiple_of((index[j, leaf] - base) * size, size)
            total = total + dot(grid[:, pl.ds(column, size)], near[leaf, j])
        for group, out in enumerate(outs):
            block = total[group * rows : (group + 1) * rows]
            out[:, leaf * part : (leaf + 1) * part] = block.astype(out.dtype)


def run_near(index, own, mate, far, edge, edge_far, relay, diag, near, after):
    rows, width = own.shape
    count, part, size = diag.shape
    return pl.pallas_call(
        near_kernel,
        in_specs=[pl.BlockSpec(memory_space=pltpu.SMEM)] + [VMEM] * 8 + [ANY],
        out_specs=[VMEM] * 4,
        out_shape=[pltpu.VMEM((rows, count * part), F32)]
        + [pltpu.VMEM((rows, count * part), BF16)] * 3,
        scratch_shapes=[pltpu.VMEM((4 * rows, width + 4 * size), BF16)],
        compiler_params=limit(12),
        cost_estimate=LIGHT,
        name="near",
    )(index, own, mate, far, edge, edge_far, relay, diag, near, after)


def settle_kernel(*refs):
    others, (turn, reach, local, leaf, final) = refs[:-5], refs[-5:]
    skel = turn.shape[1]
    total = None
    for bit, other in enumerate(others):
        term = dot3(other[:, :skel], turn[bit], TURNED)
        total = term if total is None else total + term
    leaf[...] = local[...] + dot3(total, reach[...], TURNED)
    final[...] = dot3(reach[...], turn[len(others)])


def run_settle(others, turn, reach, local):
    return pl.pallas_call(
        settle_kernel,
        in_specs=[VMEM] * (len(others) + 3),
        out_specs=[VMEM] * 2,
        out_shape=[pltpu.VMEM(local.shape, F32), pltpu.VMEM(reach.shape, F32)],
        compiler_params=limit(2),
        cost_estimate=LIGHT,
        name="settle",
    )(*others, turn, reach, local)


def last_kernel(groups, other, final, local, basis, *rest):
    close, (out_hbm, out, sems) = rest[:-3], rest[-3:]
    skel = other.shape[1]
    count = local.shape[1] // skel
    size = basis.shape[1] // count
    part = close[0].shape[1] // count
    leaf = (local[...] + dot3(other[...], final[...], TURNED)).astype(BF16)
    place = lax.axis_index("rhs")
    copies = []
    for at in range(count):
        span = slice(at * size, (at + 1) * size)
        out[:, span] = lax.dot_general(
            leaf[:, at * skel : (at + 1) * skel], basis[:, span], PLAIN, preferred_element_type=F32
        )
        for group, block in zip(groups, close):
            column = pl.multiple_of(at * size + (place ^ group) * part, part)
            here = pl.ds(column, part)
            out[:, here] = out[:, here] + block[:, at * part : (at + 1) * part].astype(F32)
        if at % 2:
            here = pl.ds((at - 1) * size, 2 * size)
            copy = pltpu.make_async_copy(out.at[:, here], out_hbm.at[:, here], sems.at[at // 2])
            copy.start()
            copies.append(copy)
    for copy in copies:
        copy.wait()


def run_last(other, final, local, basis, close):
    rows = local.shape[0]
    groups = list(close)
    return pl.pallas_call(
        functools.partial(last_kernel, groups),
        in_specs=[VMEM] * (len(close) + 4),
        out_specs=ANY,
        out_shape=jax.ShapeDtypeStruct((rows, basis.shape[1]), F32),
        scratch_shapes=[
            pltpu.VMEM((rows, basis.shape[1]), F32),
            pltpu.SemaphoreType.DMA((local.shape[1] // other.shape[1] // 2,)),
        ],
        compiler_params=limit(6),
        cost_estimate=LIGHT,
        name="last",
    )(other, final, local, basis, *close.values())


def local(
    rhs_block,
    col_basis,
    row_basis,
    leaf_transfer,
    leaf_coupling,
    inner_transfer,
    inner_coupling,
    tree_transfer,
    tree_coupling,
    diag_blocks,
    near_blocks,
    near_leaves,
):
    width = rhs_block.shape[1]
    count = leaf_transfer.shape[0]
    wide = 2 * (width // count)
    skel = col_basis.shape[0]
    span = lax.axis_size("leaf")
    ranks = lax.axis_size("rhs")
    depth = span.bit_length() - 1
    leaf_tr = leaf_transfer.reshape(count // 2, 2 * skel, skel)
    leaf_cp = leaf_coupling.reshape(count // 2, 2 * skel, skel)
    inner_tr = inner_transfer.reshape(count // 2 - 1, 2 * skel, skel)
    inner_cp = inner_coupling.reshape(count // 2 - 1, 2 * skel, skel)

    far = swapped(rhs_block, "rhs", 2)
    mate = swapped(rhs_block, "rhs", 1)
    own, tree, coeffs, second, first, block, packet, outward = run_up(
        rhs_block, col_basis, leaf_tr, inner_tr, jnp.transpose(tree_transfer, (1, 2, 0))
    )

    packet = swapped(packet, "leaf", 1)
    mats = run_pick(depth, tree)
    pairs = [(i, i + 1) for i in range(1, span - 1, 2)]
    outward = lax.ppermute(outward, "leaf", pairs + [(j, i) for i, j in pairs])
    current, other = run_first_lift(block, packet, mats, [])
    others = [other]

    def step(current, beside, width=skel):
        bit = len(others)
        others.append(swapped(current, "leaf", 1 << bit))
        return run_lift(bit, current, others[-1], mats, beside, width)

    local_part, reach = run_prep(
        coeffs,
        second,
        first,
        leaf_tr,
        leaf_cp,
        inner_tr,
        inner_cp,
        current,
    )
    current = step(current, [reach])
    edge = run_join([(packet, 2 * skel, wide), (outward, 0, wide)], [current])
    edge_far = swapped(edge, "rhs", 2)
    current = step(current, [edge])
    turn = run_turn(depth, mats, jnp.transpose(tree_coupling, (1, 2, 0)), current)
    joined = run_join(
        [(far, 0, width), (edge, 0, 2 * wide), (edge_far, 0, 2 * wide)], [current]
    )
    relay = swapped(joined, "rhs", 1)
    current = step(current, [joined, turn])
    close = run_near(
        near_leaves.T, own, mate, far, edge, edge_far, relay, diag_blocks, near_blocks, current
    )
    current = step(current, close[:1])
    close = {k: swapped(close[k], "rhs", k) if k else close[0] for k in (0, 3, 2, 1)}
    leaf_part, final = run_settle(others, turn, reach, local_part)
    other = swapped(current, "leaf", 1 << len(others))
    return run_last(other, final, leaf_part, row_basis, close)


def solution(mesh):
    in_specs = (
        P("rhs", "leaf"),
        P(None, "leaf"),
        P(None, "leaf"),
        P("leaf", None, None),
        P("leaf", None, None),
        P("leaf", None, None, None),
        P("leaf", None, None, None),
        P(),
        P(),
        P("leaf", "rhs", None),
        P("leaf", None, "rhs", None),
        P("leaf", None),
    )
    out_specs = P("rhs", "leaf")
    return jax.shard_map(local, mesh=mesh, in_specs=in_specs, out_specs=out_specs, check_vma=False)
```

```python
import functools

import jax
import jax.numpy as jnp
from jax import lax
from jax.experimental import pallas as pl
from jax.experimental.pallas import tpu as pltpu
from jax.sharding import PartitionSpec as P

F32 = jnp.float32
BF16 = jnp.bfloat16
VMEM = pl.BlockSpec(memory_space=pltpu.VMEM)
ANY = pl.BlockSpec(memory_space=pl.ANY)
PLAIN = (((1,), (0,)), ((), ()))
TURNED = (((1,), (1,)), ((), ()))


def work(flops):
    return pl.CostEstimate(flops=flops, bytes_accessed=0, transcendentals=0)


LIFT_WORK = (20_000_000_000, 500_000_000, 2_500_000_000, 20_000_000_000, 20_000_000_000)
LIGHT = work(0)


def halves(x):
    top = x.astype(BF16)
    return top, (x - top.astype(F32)).astype(BF16)


def dot3(a, b, dims=PLAIN):
    ah, al = halves(a)
    bh, bl = halves(b)
    dot = functools.partial(lax.dot_general, dimension_numbers=dims, preferred_element_type=F32)
    return dot(ah, bh) + (dot(ah, bl) + dot(al, bh))


def swapped(x, axis, bit):
    count = lax.axis_size(axis)
    return lax.ppermute(x, axis, [(i, i ^ bit) for i in range(count)])


def limit(mib):
    return pltpu.CompilerParams(vmem_limit_bytes=mib << 20)


def in_hbm(x):
    return pltpu.with_memory_space_constraint(x, pltpu.HBM)


def fetched(pairs, sems):
    copies = []
    for at, (source, target) in enumerate(pairs):
        copy = pltpu.make_async_copy(source, target, sems.at[at])
        copy.start()
        copies.append(copy)
    return copies


def up_kernel(
    rhs_hbm,
    cols_hbm,
    leaf_hbm,
    inner_hbm,
    tree_hbm,
    rhs,
    tree,
    coeffs,
    second,
    first,
    block,
    packet,
    outward,
    cols,
    leaf_tr,
    inner_tr,
    sems,
):
    size = rhs.shape[1] // 8
    wide = 2 * size
    pairs = [(rhs_hbm, rhs), (cols_hbm, cols), (leaf_hbm, leaf_tr), (inner_hbm, inner_tr), (tree_hbm, tree)]
    copies = fetched(pairs, sems)
    parts = []
    for leaf in range(8):
        if leaf == 0:
            copies[0].wait()
            copies[1].wait()
        span = slice(leaf * size, (leaf + 1) * size)
        parts.append(
            lax.dot_general(rhs[:, span], cols[:, span], TURNED, preferred_element_type=F32)
        )
    copies[2].wait()
    copies[3].wait()
    ups = []
    for pair in range(4):
        both = jnp.concatenate(parts[2 * pair : 2 * pair + 2], axis=1)
        coeffs[:, pair * 128 : (pair + 1) * 128] = both
        ups.append(dot3(both, leaf_tr[pair]))
    left = jnp.concatenate(ups[:2], axis=1)
    right = jnp.concatenate(ups[2:], axis=1)
    second[:, :128] = left
    second[:, 128:] = right
    both = jnp.concatenate([dot3(left, inner_tr[1]), dot3(right, inner_tr[2])], axis=1)
    first[...] = both
    total = dot3(both, inner_tr[0])
    block[...] = total
    packet[:, :128] = jnp.concatenate(halves(total), axis=1)
    odd = lax.rem(lax.axis_index("leaf"), 2)
    inner_side = pl.multiple_of((1 - odd) * (rhs.shape[1] - wide), wide)
    outer_side = pl.multiple_of(odd * (rhs.shape[1] - wide), wide)
    packet[:, 128:] = rhs[:, pl.ds(inner_side, wide)]
    outward[...] = rhs[:, pl.ds(outer_side, wide)]
    copies[4].wait()


def run_up(rhs, cols, leaf_tr, inner_tr, tree_tr):
    rows, width = rhs.shape
    skel = cols.shape[0]
    wide = width // 4
    tables = (cols, leaf_tr, inner_tr)
    return pl.pallas_call(
        up_kernel,
        in_specs=[ANY] * 5,
        out_specs=[VMEM] * 8,
        out_shape=[
            pltpu.VMEM(rhs.shape, rhs.dtype),
            pltpu.VMEM(tree_tr.shape, F32),
            pltpu.VMEM((rows, 8 * skel), F32),
            pltpu.VMEM((rows, 4 * skel), F32),
            pltpu.VMEM((rows, 2 * skel), F32),
            pltpu.VMEM((rows, skel), F32),
            pltpu.VMEM((rows, 2 * skel + wide), BF16),
            pltpu.VMEM((rows, wide), BF16),
        ],
        scratch_shapes=[pltpu.VMEM(x.shape, x.dtype) for x in tables]
        + [pltpu.SemaphoreType.DMA((5,))],
        compiler_params=limit(8),
        cost_estimate=LIGHT,
        name="up",
    )(*map(in_hbm, (rhs, cols, leaf_tr, inner_tr, tree_tr)))


def join_kernel(spans, *refs):
    refs, (out, sems) = refs[:-2], refs[-2:]
    pairs = []
    column = 0
    for part, (start, width) in zip(refs, spans):
        pairs.append((part.at[:, pl.ds(start, width)], out.at[:, pl.ds(column, width)]))
        column += width
    for copy in fetched(pairs, sems):
        copy.wait()


def run_join(parts, after=()):
    spans = [part[1:] for part in parts]
    arrays = [part[0] for part in parts]
    return pl.pallas_call(
        functools.partial(join_kernel, spans),
        in_specs=[ANY] * (len(parts) + len(after)),
        out_specs=VMEM,
        out_shape=pltpu.VMEM((arrays[0].shape[0], sum(w for _, w in spans)), arrays[0].dtype),
        scratch_shapes=[pltpu.SemaphoreType.DMA((len(parts),))],
        compiler_params=limit(1),
        cost_estimate=LIGHT,
        name="join",
    )(*arrays, *after)


def choose(table, wanted, picked):
    skel, _, nodes = table.shape
    select = (wanted == lax.broadcasted_iota(jnp.int32, (16, nodes), 1)).astype(BF16)
    dot = functools.partial(
        lax.dot_general, select, dimension_numbers=TURNED, preferred_element_type=F32
    )
    group = 8
    for k in range(0, skel, group):
        top, low = halves(table[k : k + group].reshape(group * skel, nodes))
        rows = dot(top) + dot(low)
        for at in range(group):
            picked[pl.ds(16 * (k + at), 16), :] = rows[:, at * skel : (at + 1) * skel]


def node_rows(nodes):
    return lax.broadcasted_iota(jnp.int32, (16, nodes), 0)


def pick_kernel(depth, tree, out, picked):
    skel, _, nodes = tree.shape
    heap = lax.axis_size("leaf") + lax.axis_index("leaf")
    row = node_rows(nodes)
    choose(tree, (lax.shift_right_logical(heap, row >> 1) ^ (row & 1)) - 2, picked)
    for bit in range(depth - 1):
        for side in range(2):
            out[bit, side * skel : (side + 1) * skel, :] = picked[
                pl.ds(2 * bit + side, skel, stride=16), :
            ]


def run_pick(depth, tree):
    skel = tree.shape[0]
    return pl.pallas_call(
        functools.partial(pick_kernel, depth),
        in_specs=[VMEM],
        out_specs=VMEM,
        out_shape=pltpu.VMEM((depth - 1, 2 * skel, skel), F32),
        scratch_shapes=[pltpu.VMEM((16 * skel, skel), F32)],
        compiler_params=limit(6),
        cost_estimate=LIGHT,
        name="pick",
    )(tree)


def first_lift_kernel(current, packet, mats, *rest):
    out, other = rest[-2:]
    skel = current.shape[1]
    sibling = packet[:, :skel].astype(F32) + packet[:, skel : 2 * skel].astype(F32)
    other[...] = sibling
    out[...] = dot3(jnp.concatenate([current[...], sibling], axis=1), mats[0])


def run_first_lift(current, packet, mats, after):
    return pl.pallas_call(
        first_lift_kernel,
        in_specs=[VMEM] * 3 + [ANY] * len(after),
        out_specs=[VMEM] * 2,
        out_shape=[pltpu.VMEM(current.shape, F32)] * 2,
        compiler_params=limit(1),
        cost_estimate=work(LIFT_WORK[0]),
        name="lift",
    )(current, packet, mats, *after)


def lift_kernel(bit, current, other, mats, *rest):
    out = rest[-1]
    skel = mats.shape[-1]
    both = jnp.concatenate([current[:, :skel], other[:, :skel]], axis=1)
    if out.shape[1] > skel:
        out[...] = jnp.zeros_like(out)
    out[:, :skel] = dot3(both, mats[bit])


def run_lift(bit, current, other, mats, after, width):
    return pl.pallas_call(
        functools.partial(lift_kernel, bit),
        in_specs=[VMEM] * 3 + [ANY] * len(after),
        out_specs=VMEM,
        out_shape=pltpu.VMEM((current.shape[0], width), F32),
        compiler_params=limit(1),
        cost_estimate=work(LIFT_WORK[bit]),
        name="lift",
    )(current, other, mats, *after)


def prep_kernel(
    coeffs,
    second,
    first,
    after,
    leaf_tr_hbm,
    leaf_cp_hbm,
    inner_tr_hbm,
    inner_cp_hbm,
    local_ref,
    reach_ref,
    leaf_tr,
    leaf_cp,
    inner_tr,
    inner_cp,
    sems,
):
    del after
    copies = fetched(
        [
            (inner_cp_hbm, inner_cp),
            (inner_tr_hbm, inner_tr),
            (leaf_cp_hbm, leaf_cp),
            (leaf_tr_hbm, leaf_tr),
        ],
        sems,
    )

    def coupled(values, table):
        rows = values.shape[0]
        both = dot3(jnp.concatenate([values[:, 64:], values[:, :64]], axis=0), table, TURNED)
        return jnp.concatenate([both[:rows, :64], both[rows:, 64:]], axis=1)

    for copy in copies:
        copy.wait()
    tops = coupled(first[...], inner_cp[0])
    mids = []
    for side in range(2):
        own = coupled(second[:, side * 128 : (side + 1) * 128], inner_cp[1 + side])
        mids.append(own + dot3(tops[:, side * 64 : (side + 1) * 64], inner_tr[1 + side], TURNED))
    reach_top = inner_tr[0]
    for pair in range(4):
        side = pair // 2
        low = (pair % 2) * 64
        own = coupled(coeffs[:, pair * 128 : (pair + 1) * 128], leaf_cp[pair])
        own = own + dot3(mids[side][:, low : low + 64], leaf_tr[pair], TURNED)
        local_ref[:, pair * 128 : (pair + 1) * 128] = own
        if pair % 2 == 0:
            reach_mid = dot3(inner_tr[1 + side], reach_top[side * 64 : (side + 1) * 64])
        reach_ref[pair * 128 : (pair + 1) * 128, :] = dot3(leaf_tr[pair], reach_mid[low : low + 64])


def run_prep(coeffs, second, first, leaf_tr, leaf_cp, inner_tr, inner_cp, after):
    rows = coeffs.shape[0]
    skel = first.shape[1] // 2
    tables = (leaf_tr, leaf_cp, inner_tr, inner_cp)
    return pl.pallas_call(
        prep_kernel,
        in_specs=[VMEM] * 3 + [ANY] * 5,
        out_specs=[VMEM] * 2,
        out_shape=[
            pltpu.VMEM((rows, 8 * skel), F32),
            pltpu.VMEM((8 * skel, skel), F32),
        ],
        scratch_shapes=[pltpu.VMEM(x.shape, F32) for x in tables] + [pltpu.SemaphoreType.DMA((4,))],
        compiler_params=limit(6),
        cost_estimate=LIGHT,
        name="prep",
    )(coeffs, second, first, after, *map(in_hbm, tables))


def turn_kernel(depth, mats, tree, after, out, picked):
    del after
    skel, _, nodes = tree.shape
    heap = lax.axis_size("leaf") + lax.axis_index("leaf")
    choose(tree, lax.shift_right_logical(heap, node_rows(nodes)) - 2, picked)
    chain = None
    for bit in range(depth):
        couple = picked[pl.ds(bit, skel, stride=16), :]
        out[bit] = couple if chain is None else dot3(chain, couple)
        if bit + 1 < depth:
            step = mats[bit, :skel]
            chain = step if chain is None else dot3(chain, step)


def run_turn(depth, mats, tree, after):
    skel = tree.shape[0]
    return pl.pallas_call(
        functools.partial(turn_kernel, depth),
        in_specs=[VMEM] * 2 + [ANY],
        out_specs=VMEM,
        out_shape=pltpu.VMEM((depth, skel, skel), F32),
        scratch_shapes=[pltpu.VMEM((16 * skel, skel), F32)],
        compiler_params=limit(6),
        cost_estimate=LIGHT,
        name="turn",
    )(mats, tree, after)


def near_kernel(index, own, mate, far, edge, edge_far, relay, diag, near, after, *rest):
    del after
    outs, grid = rest[:4], rest[4]
    rows, width = own.shape
    count, part, size = diag.shape
    wide = 2 * size
    odd = lax.rem(lax.axis_index("leaf"), 2)
    inner = pl.multiple_of((1 - odd) * (width + wide), wide)
    outer = pl.multiple_of(odd * (width + wide), wide)

    def place(source, start, length, group, column):
        target = (pl.ds(group * rows, rows), pl.ds(column, length))
        grid[target] = source[:, start : start + length]

    place(own, 0, width, 0, wide)
    place(mate, 0, width, 1, wide)
    place(far, 0, width, 2, wide)
    place(relay, 0, width, 3, wide)
    for group, (source, start) in enumerate(
        ((edge, 0), (relay, width), (edge_far, 0), (relay, width + 2 * wide))
    ):
        place(source, start, wide, group, inner)
        place(source, start + wide, wide, group, outer)
    base = lax.axis_index("leaf") * count - 2
    dot = functools.partial(
        lax.dot_general, dimension_numbers=TURNED, preferred_element_type=F32
    )
    for leaf in range(count):
        total = dot(grid[:, (leaf + 2) * size : (leaf + 3) * size], diag[leaf])
        for j in range(near.shape[1]):
            column = pl.multiple_of((index[j, leaf] - base) * size, size)
            total = total + dot(grid[:, pl.ds(column, size)], near[leaf, j])
        for group, out in enumerate(outs):
            block = total[group * rows : (group + 1) * rows]
            out[:, leaf * part : (leaf + 1) * part] = block.astype(out.dtype)


def run_near(index, own, mate, far, edge, edge_far, relay, diag, near, after):
    rows, width = own.shape
    count, part, size = diag.shape
    return pl.pallas_call(
        near_kernel,
        in_specs=[pl.BlockSpec(memory_space=pltpu.SMEM)] + [VMEM] * 8 + [ANY],
        out_specs=[VMEM] * 4,
        out_shape=[pltpu.VMEM((rows, count * part), F32)]
        + [pltpu.VMEM((rows, count * part), BF16)] * 3,
        scratch_shapes=[pltpu.VMEM((4 * rows, width + 4 * size), BF16)],
        compiler_params=limit(12),
        cost_estimate=LIGHT,
        name="near",
    )(index, own, mate, far, edge, edge_far, relay, diag, near, after)


def settle_kernel(*refs):
    others, (turn, reach, local, leaf, final) = refs[:-5], refs[-5:]
    skel = turn.shape[1]
    total = None
    for bit, other in enumerate(others):
        term = dot3(other[:, :skel], turn[bit], TURNED)
        total = term if total is None else total + term
    leaf[...] = local[...] + dot3(total, reach[...], TURNED)
    final[...] = dot3(reach[...], turn[len(others)])


def run_settle(others, turn, reach, local):
    return pl.pallas_call(
        settle_kernel,
        in_specs=[VMEM] * (len(others) + 3),
        out_specs=[VMEM] * 2,
        out_shape=[pltpu.VMEM(local.shape, F32), pltpu.VMEM(reach.shape, F32)],
        compiler_params=limit(2),
        cost_estimate=LIGHT,
        name="settle",
    )(*others, turn, reach, local)


def last_kernel(groups, other, final, local, basis, *rest):
    close, (out_hbm, out, sems) = rest[:-3], rest[-3:]
    skel = other.shape[1]
    count = local.shape[1] // skel
    size = basis.shape[1] // count
    part = close[0].shape[1] // count
    leaf = (local[...] + dot3(other[...], final[...], TURNED)).astype(BF16)
    place = lax.axis_index("rhs")
    copies = []
    for at in range(count):
        span = slice(at * size, (at + 1) * size)
        out[:, span] = lax.dot_general(
            leaf[:, at * skel : (at + 1) * skel], basis[:, span], PLAIN, preferred_element_type=F32
        )
        for group, block in zip(groups, close):
            column = pl.multiple_of(at * size + (place ^ group) * part, part)
            here = pl.ds(column, part)
            out[:, here] = out[:, here] + block[:, at * part : (at + 1) * part].astype(F32)
        if at % 2:
            here = pl.ds((at - 1) * size, 2 * size)
            copy = pltpu.make_async_copy(out.at[:, here], out_hbm.at[:, here], sems.at[at // 2])
            copy.start()
            copies.append(copy)
    for copy in copies:
        copy.wait()


def run_last(other, final, local, basis, close):
    rows = local.shape[0]
    groups = list(close)
    return pl.pallas_call(
        functools.partial(last_kernel, groups),
        in_specs=[VMEM] * (len(close) + 4),
        out_specs=ANY,
        out_shape=jax.ShapeDtypeStruct((rows, basis.shape[1]), F32),
        scratch_shapes=[
            pltpu.VMEM((rows, basis.shape[1]), F32),
            pltpu.SemaphoreType.DMA((local.shape[1] // other.shape[1] // 2,)),
        ],
        compiler_params=limit(6),
        cost_estimate=LIGHT,
        name="last",
    )(other, final, local, basis, *close.values())


def local(
    rhs_block,
    col_basis,
    row_basis,
    leaf_transfer,
    leaf_coupling,
    inner_transfer,
    inner_coupling,
    tree_transfer,
    tree_coupling,
    diag_blocks,
    near_blocks,
    near_leaves,
):
    width = rhs_block.shape[1]
    count = leaf_transfer.shape[0]
    wide = 2 * (width // count)
    skel = col_basis.shape[0]
    span = lax.axis_size("leaf")
    ranks = lax.axis_size("rhs")
    depth = span.bit_length() - 1
    leaf_tr = leaf_transfer.reshape(count // 2, 2 * skel, skel)
    leaf_cp = leaf_coupling.reshape(count // 2, 2 * skel, skel)
    inner_tr = inner_transfer.reshape(count // 2 - 1, 2 * skel, skel)
    inner_cp = inner_coupling.reshape(count // 2 - 1, 2 * skel, skel)

    far = swapped(rhs_block, "rhs", 2)
    mate = swapped(rhs_block, "rhs", 1)
    own, tree, coeffs, second, first, block, packet, outward = run_up(
        rhs_block, col_basis, leaf_tr, inner_tr, jnp.transpose(tree_transfer, (1, 2, 0))
    )

    packet = swapped(packet, "leaf", 1)
    mats = run_pick(depth, tree)
    pairs = [(i, i + 1) for i in range(1, span - 1, 2)]
    outward = lax.ppermute(outward, "leaf", pairs + [(j, i) for i, j in pairs])
    current, other = run_first_lift(block, packet, mats, [])
    others = [other]

    def step(current, beside, width=skel):
        bit = len(others)
        others.append(swapped(current, "leaf", 1 << bit))
        return run_lift(bit, current, others[-1], mats, beside, width)

    local_part, reach = run_prep(
        coeffs,
        second,
        first,
        leaf_tr,
        leaf_cp,
        inner_tr,
        inner_cp,
        current,
    )
    current = step(current, [reach])
    edge = run_join([(packet, 2 * skel, wide), (outward, 0, wide)], [current])
    edge_far = swapped(edge, "rhs", 2)
    current = step(current, [edge])
    turn = run_turn(depth, mats, jnp.transpose(tree_coupling, (1, 2, 0)), current)
    joined = run_join(
        [(far, 0, width), (edge, 0, 2 * wide), (edge_far, 0, 2 * wide)], [current]
    )
    relay = swapped(joined, "rhs", 1)
    current = step(current, [joined, turn])
    close = run_near(
        near_leaves.T, own, mate, far, edge, edge_far, relay, diag_blocks, near_blocks, current
    )
    current = step(current, close[:1])
    close = {k: swapped(close[k], "rhs", k) if k else close[0] for k in (0, 3, 2, 1)}
    leaf_part, final = run_settle(others, turn, reach, local_part)
    other = swapped(current, "leaf", 1 << len(others))
    return run_last(other, final, leaf_part, row_basis, close)


def solution(mesh):
    in_specs = (
        P("rhs", "leaf"),
        P(None, "leaf"),
        P(None, "leaf"),
        P("leaf", None, None),
        P("leaf", None, None),
        P("leaf", None, None, None),
        P("leaf", None, None, None),
        P(),
        P(),
        P("leaf", "rhs", None),
        P("leaf", None, "rhs", None),
        P("leaf", None),
    )
    out_specs = P("rhs", "leaf")
    return jax.shard_map(local, mesh=mesh, in_specs=in_specs, out_specs=out_specs, check_vma=False)
```
